256 devices in a mesh: dp: 32 (over z, x), seq: 4 (over y), tensor: 2 (over core).
Axes of the slice: x: 4, y: 4, z: 8, core: 2. Of those that a mesh axis runs over, the one named last changes fastest.
Arguments:
- patches: bfloat16 [16384, 1280], P(('dp', 'seq')), may hold values from -1.796875 to 1.796875
- arrivals: int32 [128, 32], P(('dp', 'seq')), may hold values from 2 to 4, as said below
- segment_ids: int32 [16384], P('dp'), may hold values from -1 to 63, as said below
- norm_gain: float32 [1280], replicated, may hold values from 0.25 to 1.75
- norm_bias: float32 [1280], replicated, may hold values from -3 to 3
- w_qkv: bfloat16 [1280, 3840], P(None, 'tensor')
- w_out: bfloat16 [1280, 1280], P('tensor'), may hold values from -0.625 to 0.625
- grad_out: bfloat16 [16384, 1280], P(('dp', 'seq')), may hold values from -0.1875 to 0.1875
Outputs:
- layer_out: bfloat16 [16384, 1280], P(('dp', 'seq'))
- grad_qkv: float32 [1280, 3840], P(('dp', 'seq'), 'tensor')
- grad_wout: float32 [1280, 1280], P(('dp', 'seq'), 'tensor')
The draws below stay inside these ranges and needn't reach their ends.
Inputs may be any that keep to these rules, and one draw needn't show every extreme that they name: `arrivals`: for each receiver the counts from the 32 sources differ by at most one; in every draw some receiver gets 4 from every source and some gets 4 // 2 from every source. `segment_ids`: packed row r * 128 + t has id -1 exactly when t is not below the sum of arrivals[r]; within one dp shard's rows the other ids never fall and lie in j * 2 to j * 2 + 1 for dp shard j.
All inputs are finite; a program needn't handle non-finite values.
Results may differ from the reference program's by a relative error of at most 0.015.
Values may be sent and summed in bfloat16 or wider, within the bound.
A program may use at most 128 MiB of HBM per device.

```python
import jax
import jax.numpy as jnp
from jax import lax

D = 1280
HEADS = 16
HEAD = 80
TOK_DEV = 128
IMG_OWN = 2
CAP = 4
TOKENS = 16384
N_DP = 32
N_SEQ = 4


def valid_rows(key):
    senders = N_DP * N_SEQ
    counts = jax.random.randint(jax.random.fold_in(key, 1), (senders,), TOK_DEV // 2, TOK_DEV + 1)
    filled = jax.random.randint(jax.random.fold_in(key, 2), (), 0, senders)
    places = jnp.arange(senders)
    counts = jnp.where(places == filled, TOK_DEV, counts)
    counts = jnp.where(places == (filled + 1) % senders, TOK_DEV // 2, counts)
    return counts.astype(jnp.int32)


def one_order(subkey):
    return jax.random.permutation(subkey, N_DP)


def draw_arrivals(key, part):
    row_count = valid_rows(key)
    key = jax.random.fold_in(key, 11)
    orders = jax.vmap(one_order)(jax.random.split(key, N_DP * N_SEQ))
    surplus = (orders < (row_count % N_DP)[:, None]).astype(jnp.int32)
    return ((row_count // N_DP)[:, None] + surplus).astype(jnp.int32)


def draw_segment_ids(key, part):
    row_count = valid_rows(key)
    key = jax.random.fold_in(key, 12)
    places = jnp.arange(TOK_DEV, dtype=jnp.int32)
    occupied = (places[None, :] < row_count[:, None]).reshape(N_DP, N_SEQ * TOK_DEV)
    ordinal = jnp.cumsum(occupied.astype(jnp.int32), axis=1, dtype=jnp.int32) - 1
    owned_rows = jnp.sum(occupied.astype(jnp.int32), axis=1, dtype=jnp.int32)
    boundary = jax.random.randint(key, (N_DP, IMG_OWN - 1), 1, owned_rows[:, None])
    image_rank = jnp.sum((ordinal[:, :, None] >= boundary[:, None, :]).astype(jnp.int32), axis=2, dtype=jnp.int32)
    owners = jnp.arange(N_DP, dtype=jnp.int32)[:, None] * IMG_OWN
    return jnp.where(occupied, owners + image_rank, -1).reshape(N_DP * N_SEQ * TOK_DEV).astype(jnp.int32)


def draw_w_qkv(key, part):
    key = jax.random.fold_in(key, 13)
    matrix = jax.random.normal(jax.random.fold_in(key, 1), (D, HEADS, 3, HEAD), jnp.float32) * D ** (-0.5)
    return matrix.reshape(D, 3 * D).astype(jnp.bfloat16)


def strengthened(values, key, source, target, shards_of, factor):
    def block_of(axis_at):
        return (jnp.arange(values.shape[axis_at]) // (values.shape[axis_at] // shards_of)).reshape((-1,) + (1,) * (values.ndim - 1 - axis_at))

    first = jax.random.permutation(key, shards_of)[block_of(target)]
    far = (block_of(target) + shards_of // 2) % shards_of
    return jnp.where((block_of(source) == first) | (block_of(source) == far), factor * values, values)


def levels(stream_key, extent, cuts, low, top_value):
    level = 1.0
    for dim, shards_of in cuts:
        draws = jax.random.uniform(jax.random.fold_in(jax.random.fold_in(stream_key, 6), dim), (shards_of,), jnp.float32, low / len(cuts), top_value / len(cuts))
        level = level * jnp.repeat(jnp.exp(draws), extent[dim] // shards_of).reshape((-1,) + (1,) * (len(extent) - 1 - dim))
    return level


def scatter_about(own_key, shape, deviation, limit, shards=(), held_as=jnp.bfloat16):
    drawn = jax.random.normal(own_key, shape, jnp.float32) * deviation
    if len(shards) > 0:
        drawn = levels(own_key, shape, shards, -0.22, 0.18) * drawn
    return jnp.clip(drawn, min=-limit, max=limit).astype(held_as)


def gaussian_with(own_key, shape, scale, most, cuts, heavy, kind=jnp.bfloat16):
    drawn = scale * jax.random.normal(own_key, shape, jnp.float32)
    if cuts:
        drawn = drawn * levels(own_key, shape, cuts, -0.22, 0.18)
    return jnp.clip(strengthened(drawn, jax.random.fold_in(own_key, 3), *heavy), -most, most).astype(kind)


def setup_inputs(seed: int = 0) -> dict:
    seeds = jax.random.split(jax.random.key(seed), 9)
    patches = scatter_about(seeds[0], (TOKENS, D), 0.3, 1.796875, ((0, 128),))
    arrivals = draw_arrivals(jax.random.fold_in(seeds[8], 71), 0)
    segment_ids = draw_segment_ids(jax.random.fold_in(seeds[8], 71), 0)
    norm_gain = jnp.clip(1.0 + 0.15 * jax.random.normal(seeds[3], (D,), jnp.float32), 0.25, 1.75)
    norm_bias = scatter_about(seeds[4], (D,), 0.5, 3.0, (), jnp.float32)
    w_qkv = draw_w_qkv(jax.random.fold_in(seeds[8], 71), 0)
    w_out = scatter_about(seeds[6], (D, D), (D // 16) ** -0.5, 0.625, ((0, 2),))
    grad_out = gaussian_with(seeds[7], (TOKENS, D), (TOKENS ** -0.5), 0.1875, ((0, 128),), (0, 1, 128, 5.5))
    return {"patches": patches, "arrivals": arrivals, "segment_ids": segment_ids, "norm_gain": norm_gain, "norm_bias": norm_bias, "w_qkv": w_qkv, "w_out": w_out, "grad_out": grad_out}


epsilon = 1e-06
big_negative = -1e+30

def weights_of(scores, allowed, valid_query):
    masked = jnp.where(allowed, scores, big_negative)
    row_max = lax.optimization_barrier(jnp.max(masked, axis=1, keepdims=True))
    raised = jnp.where(allowed, jnp.exp(masked - row_max), 0.0)
    head_total = jnp.where(valid_query, lax.optimization_barrier(jnp.sum(raised, axis=1)), 1.0)
    return raised / head_total[:, None]

def pack_rows(patches, arrivals):
    slots = patches.reshape(N_DP, N_SEQ, N_DP, CAP, D).transpose(2, 1, 0, 3, 4).reshape(N_DP * N_SEQ, N_DP * CAP, D)

    def receive(received, counts):
        run_ends = jnp.cumsum(counts, dtype=jnp.int32)
        starts = run_ends - counts
        position = jnp.arange(TOK_DEV, dtype=jnp.int32)
        source = jnp.minimum(lax.optimization_barrier(jnp.sum((run_ends[None, :] <= position[:, None]).astype(jnp.int32), axis=1, dtype=jnp.int32)), N_DP - 1)
        slot_index = jnp.clip(source * CAP + position - starts[source], 0, TOK_DEV - 1)
        picked = jnp.take(received, slot_index, axis=0)
        return jnp.where((position < run_ends[N_DP - 1])[:, None], picked, jnp.zeros_like(picked))
    return jax.vmap(receive)(slots, arrivals)

def group_pass(packed, segments, cotangent, norm_gain, norm_bias, w_qkv, w_out):
    group_rows = packed.shape[0]
    score_scale = HEAD ** (-0.5)
    residual = packed.astype(jnp.float32)
    centre = residual - lax.optimization_barrier(jnp.mean(residual, axis=1, keepdims=True))
    spread = lax.optimization_barrier(jnp.mean(centre * centre, axis=1, keepdims=True))
    normed = (centre * lax.rsqrt(spread + epsilon) * norm_gain + norm_bias).astype(jnp.bfloat16)
    projected = jnp.dot(normed, w_qkv, preferred_element_type=jnp.float32).astype(jnp.bfloat16)
    pieces = projected.reshape(group_rows, HEADS, 3, HEAD).transpose(1, 2, 0, 3)
    allowed = (segments[:, None] == segments[None, :]) & (segments[None, :] >= 0)
    valid_query = segments >= 0

    def forward_head(triple):
        scores = jnp.dot(triple[0], triple[1].T, preferred_element_type=jnp.float32) * score_scale
        weights = weights_of(scores, allowed, valid_query).astype(jnp.bfloat16)
        return jnp.dot(weights, triple[2], preferred_element_type=jnp.float32).astype(jnp.bfloat16)
    attended_heads = lax.map(forward_head, pieces)
    attended = attended_heads.transpose(1, 0, 2).reshape(group_rows, D)
    mixing = jnp.dot(attended, w_out, preferred_element_type=jnp.float32)
    layer_out = (residual + mixing).astype(jnp.bfloat16)
    d_attended = jnp.dot(cotangent, w_out.T, preferred_element_type=jnp.float32).astype(jnp.bfloat16)
    grad_heads = d_attended.reshape(group_rows, HEADS, HEAD).transpose(1, 0, 2)

    def backward_head(operands):
        triple, head_out, head_grad = operands
        scores = jnp.dot(triple[0], triple[1].T, preferred_element_type=jnp.float32) * score_scale
        exact = weights_of(scores, allowed, valid_query)
        weights = exact.astype(jnp.bfloat16)
        d_weights = jnp.dot(head_grad, triple[2].T, preferred_element_type=jnp.float32)
        delta_row = lax.optimization_barrier(jnp.sum(head_grad.astype(jnp.float32) * head_out.astype(jnp.float32), axis=1, keepdims=True))
        d_scores = (exact * (d_weights - delta_row) * score_scale).astype(jnp.bfloat16)
        d_query = jnp.dot(d_scores, triple[1], preferred_element_type=jnp.float32).astype(jnp.bfloat16)
        d_key = jnp.dot(d_scores.T, triple[0], preferred_element_type=jnp.float32).astype(jnp.bfloat16)
        d_value = jnp.dot(weights.T, head_grad, preferred_element_type=jnp.float32).astype(jnp.bfloat16)
        return jnp.stack([d_query, d_key, d_value], axis=0)
    head_grads = lax.map(backward_head, (pieces, attended_heads, grad_heads))
    projection_grads = head_grads.transpose(2, 0, 1, 3).reshape(group_rows, 3 * D)
    term_qkv = jnp.dot(normed.T, projection_grads, preferred_element_type=jnp.float32)
    term_out = jnp.dot(cotangent.T, attended, preferred_element_type=jnp.float32)
    return (layer_out, term_qkv, term_out)

def reference(patches, arrivals, segment_ids, norm_gain, norm_bias, w_qkv, w_out, grad_out):
    packed = pack_rows(patches, arrivals).reshape(N_DP, N_SEQ * TOK_DEV, D)
    segments = segment_ids.reshape(N_DP, N_SEQ * TOK_DEV)
    cotangent = grad_out.reshape(N_DP, N_SEQ * TOK_DEV, D)

    def accumulate(carry, inputs):
        layer_out, term_qkv, term_out = group_pass(inputs[0], inputs[1], inputs[2], norm_gain, norm_bias, w_qkv, w_out)
        return ((carry[0] + term_qkv, carry[1] + term_out), layer_out)
    zeros_pair = (jnp.zeros((D, 3 * D), jnp.float32), jnp.zeros((D, D), jnp.float32))
    summed, outputs = lax.scan(accumulate, zeros_pair, (packed, segments, cotangent))
    return (outputs.reshape(N_DP * N_SEQ * TOK_DEV, D), summed[0], summed[1])
```

```python
import functools

import jax
import jax.numpy as jnp
from jax import lax
from jax.experimental import pallas as pl
from jax.experimental.pallas import tpu as pltpu
from jax.sharding import PartitionSpec as P

HEAD = 80
PAD = 128
HEADS_OWN = 2
NX = 4
NS = 4
ROWS = 128
D = 1280
HALF = D // 2
GROUP = NS * ROWS
QKV = 3 * HEADS_OWN * HEAD
ATT = HEADS_OWN * PAD
SPLIT = 256
COLS = 4 * HEADS_OWN * HEAD
CHUNK = 160
OWN = 40
SLOT = 48
FINAL = 16
epsilon = 1e-06
big_negative = -1e30
MESH = pl.DeviceIdType.MESH
bf16 = jnp.bfloat16
f32 = jnp.float32


def nn(a, b):
    return jnp.dot(a, b, preferred_element_type=f32)


def nt(a, b):
    return lax.dot_general(a, b, (((1,), (1,)), ((), ())), preferred_element_type=f32)


def iota(shape, axis):
    return lax.broadcasted_iota(jnp.int32, shape, axis)


def kernel(nz, patches, arrivals, seg, gain, bias, w_qkv, w_out, gout, layer_out, grads, *scratch):
    (az, xs_out, ax, pk, nrm, gall, w_win, w_pad, wo_pad, proj, n_t, go_t, ga, ga_t, segk,
     pt_n, pt_g, pn1, pg1, pg2, pn2, att, att_all, lo_out, lo_in,
     rs_out1, rs_in1, rs_out2, rs_in2, x_out1, x_in1, x_out2, x_in2, z_sum1, z_sum2,
     y_out1, y_in1, y_out2, y_in2,
     loc, az_s, az_r, gy_s, gy_r, gf_s, gf_r, ax_s, ax_r, pk_s, pk_r, ny_s, ny_r, nf_s, nf_r,
     at_s, at_r, lo_s, lo_r, rs_s, rs_r, x_s, x_r, y_s, y_r) = scratch
    dp, s, c = lax.axis_index("dp"), lax.axis_index("seq"), lax.axis_index("tensor")
    z, x = lax.div(dp, NX), lax.rem(dp, NX)
    started = []

    def at_z(zt):
        return {"dp": lax.rem(zt + nz, nz) * NX + x}

    def at_x(xt):
        return {"dp": z * NX + lax.rem(xt + NX, NX)}

    def at_s_(st):
        return {"seq": lax.rem(st + NS, NS)}

    other = {"tensor": 1 - c}

    def send(src, dst, ssem, rsem, device):
        copy = pltpu.make_async_remote_copy(
            src_ref=src, dst_ref=dst, send_sem=ssem, recv_sem=rsem, device_id=device,
            device_id_type=MESH,
        )
        copy.start()
        started.append(copy)
        return copy

    def fetch(src, dst, sem):
        copy = pltpu.make_async_copy(src, dst, sem)
        copy.start()
        return copy

    cols = pl.ds(pl.multiple_of(c * HALF, HALF), HALF)
    mine = pl.ds(pl.multiple_of(s * ROWS, ROWS), ROWS)

    own_patch = fetch(
        patches.at[pl.ds(pl.multiple_of(z * 16, 16), 16), cols],
        az.at[pl.ds(pl.multiple_of(z * 16, 16), 16)], loc.at[0],
    )
    own_gout = [
        fetch(gout.at[:, pl.ds(i * HALF, HALF)], gall.at[i, mine], loc.at[1 + i]) for i in range(2)
    ]
    w_start = lax.min(lax.div(QKV * s, 128) * 128, 3 * D // 2 - HALF)
    w_off = QKV * s - w_start
    w_copy = fetch(w_qkv.at[:, pl.ds(pl.multiple_of(w_start, 128), HALF)], w_win, loc.at[3])
    wo_copies = [
        fetch(w_out.at[pl.ds(i * HEAD, HEAD)], wo_pad.at[pl.ds(i * PAD, HEAD)], loc.at[4 + i])
        for i in range(NS * HEADS_OWN)
    ]

    barrier = pltpu.get_barrier_semaphore()
    partners = (
        [at_z(z + k) for k in range(1, nz)]
        + [at_x(x + k) for k in range(1, NX)]
        + [at_s_(s + k) for k in range(1, NS)]
        + [other]
    )
    for device in partners:
        pl.semaphore_signal(barrier, inc=1, device_id=device, device_id_type=MESH)
    pl.semaphore_wait(barrier, len(partners))

    az_copies = []
    for k in range(1, nz):
        zt = lax.rem(z + k, nz)
        az_copies.append(send(
            patches.at[pl.ds(pl.multiple_of(zt * 16, 16), 16), cols],
            az.at[pl.ds(pl.multiple_of(z * 16, 16), 16)],
            az_s.at[k - 1], az_r.at[k - 1], at_z(z + k),
        ))
    gy_copies = {
        k: send(gout.at[:, cols], gall.at[c, mine], gy_s.at[k - 1], gy_r.at[k - 1], at_s_(s + k))
        for k in (1, 3, 2)
    }

    row, col = iota((ROWS, ROWS), 0), iota((ROWS, ROWS), 1)
    source_row = ((row >> 2) & 7) * 16 + (row >> 5) * 4 + (row & 3)
    perm = (col == source_row).astype(bf16)
    slot = iota((32, ROWS), 1)
    origin = ((slot >> 2) & 7) * NX + (slot >> 5)
    counter = iota((32, ROWS), 0)
    counts = jnp.broadcast_to(arrivals[...].astype(f32), (16, 32)).astype(bf16)
    starts = nn(counts, (counter < origin).astype(bf16))[0:1]
    number = nn(counts, (counter == origin).astype(bf16))[0:1]
    place = (iota((1, ROWS), 1) & 3).astype(f32)
    target = jnp.where(place < number, starts + place, -1.0)
    pick = (row.astype(f32) == target).astype(bf16)

    ids = seg[...].astype(f32)
    key_ids = jnp.where(ids < 0.0, -2.0, ids)
    segk[...] = jnp.broadcast_to(key_ids, (PAD, GROUP)).T

    for i in range(NS * HEADS_OWN):
        wo_pad[i * PAD + HEAD:(i + 1) * PAD] = jnp.zeros((PAD - HEAD, D), bf16)
    pt_n[3 * HEAD:5 * HEAD] = jnp.zeros((2 * HEAD, GROUP), bf16)
    pt_g[...] = jnp.zeros(pt_g.shape, bf16)

    w_copy.wait()

    def pad_pair(i, carry):
        r, cc = iota((HALF, 2 * PAD), 0), iota((HALF, 2 * PAD), 1)
        d = cc & (PAD - 1)
        wanted = w_off + (2 * i + (cc >> 7)) * HEAD + d
        chosen = ((r == wanted) & (d < HEAD)).astype(bf16)
        out = pl.ds(pl.multiple_of(i * 2 * PAD, 2 * PAD), 2 * PAD)
        w_pad[:, out] = nn(w_win[...], chosen).astype(bf16)
        return carry

    lax.fori_loop(0, 3, pad_pair, 0)
    for copy in wo_copies:
        copy.wait()

    own_patch.wait()
    for copy in az_copies:
        copy.wait_recv()
    xs_out[...] = nn(perm, az[...]).astype(bf16)
    slots_x = pl.ds(pl.multiple_of(x * 32, 32), 32)
    ax_copies = []
    for k in range(1, NX):
        xt = lax.rem(x + k, NX)
        ax_copies.append(send(
            xs_out.at[pl.ds(pl.multiple_of(xt * 32, 32), 32)], ax.at[slots_x],
            ax_s.at[k - 1], ax_r.at[k - 1], at_x(x + k),
        ))
    ax[slots_x] = xs_out[slots_x]
    for copy in ax_copies:
        copy.wait_recv()
    pk[c] = nn(pick, ax[...]).astype(bf16)
    pk_copy = send(pk.at[c], pk.at[c], pk_s, pk_r, other)
    pk_copy.wait_recv()

    x0, x1 = pk[0].astype(f32), pk[1].astype(f32)
    mean = (jnp.sum(x0, axis=1, keepdims=True) + jnp.sum(x1, axis=1, keepdims=True)) / D
    x0, x1 = x0 - mean, x1 - mean
    var = (jnp.sum(x0 * x0, axis=1, keepdims=True) + jnp.sum(x1 * x1, axis=1, keepdims=True)) / D
    inv = lax.rsqrt(var + epsilon)
    nrm[0, mine] = (x0 * inv * gain[:, :HALF] + bias[:, :HALF]).astype(bf16)
    nrm[1, mine] = (x1 * inv * gain[:, HALF:] + bias[:, HALF:]).astype(bf16)
    ny_copies = {
        k: send(nrm.at[c, mine], nrm.at[c, mine], ny_s.at[k - 1], ny_r.at[k - 1], at_s_(s + k))
        for k in (1, 3, 2)
    }

    def project(start):
        block = pl.ds(pl.multiple_of(start, ROWS), ROWS)
        b0, b1 = nrm[0, block], nrm[1, block]
        proj[block] = (nn(b0, w_pad[:HALF]) + nn(b1, w_pad[HALF:])).astype(bf16)
        n_t[:HALF, block] = b0.T
        n_t[HALF:, block] = b1.T

    def peer_rows(k):
        return pl.multiple_of(lax.rem(s + NS - k, NS) * ROWS, ROWS)

    gf_copies = []
    for k in (1, 3, 2):
        gy_copies[k].wait_recv()
        block = pl.ds(peer_rows(k), ROWS)
        gf_copies.append(send(
            gall.at[c, block], gall.at[c, block], gf_s.at[k - 1], gf_r.at[k - 1], other
        ))
    project(s * ROWS)
    for copy in own_gout:
        copy.wait()
    for copy in gf_copies:
        copy.wait_recv()
    wo_mine = wo_pad[pl.ds(pl.multiple_of(s * ATT, ATT), ATT)]
    ga[...] = (nt(gall[0], wo_mine[:, :HALF]) + nt(gall[1], wo_mine[:, HALF:])).astype(bf16)
    ga_t[...] = (nt(wo_mine[:, :HALF], gall[0]) + nt(wo_mine[:, HALF:], gall[1])).astype(bf16)
    go_t[:HALF] = gall[0].T
    go_t[HALF:] = gall[1].T

    nf_copies = {}

    def pass_on(k):
        ny_copies[k].wait_recv()
        block = pl.ds(peer_rows(k), ROWS)
        nf_copies[k] = send(
            nrm.at[c, block], nrm.at[c, block], nf_s.at[k - 1], nf_r.at[k - 1], other
        )

    def take(k):
        nf_copies[k].wait_recv()
        project(peer_rows(k))

    pass_on(1)
    pass_on(3)
    take(1)
    take(3)
    pass_on(2)
    take(2)

    scale = HEAD ** (-0.5)
    to_exp2 = scale * 1.4426950408889634
    query_ids = ids

    def head(h):
        base = 3 * PAD * h
        k_, v_ = proj[:, base + PAD:base + 2 * PAD], proj[:, base + 2 * PAD:base + 3 * PAD]
        k_t, v_t = k_.T, v_.T
        d_k = jnp.zeros((GROUP, PAD), f32)
        d_v = jnp.zeros((GROUP, PAD), f32)
        wide = 256
        for b in range(GROUP // wide):
            part = slice(b * wide, (b + 1) * wide)
            q_ = proj[part, base:base + PAD]
            g_ = ga[part, h * PAD:(h + 1) * PAD]
            g_t = ga_t[h * PAD:(h + 1) * PAD, part]
            scores = nt(k_, q_)
            keys = jnp.concatenate([segk[...]] * (wide // PAD), axis=1)
            masked = jnp.where(keys == query_ids[:, part], scores, big_negative)
            top = jnp.max(masked, axis=0, keepdims=True)
            raised = jnp.exp2((masked - top) * to_exp2)
            total = jnp.sum(raised, axis=0, keepdims=True)
            share = jnp.where(query_ids[:, part] < 0.0, 0.0, 1.0 / total)
            exact = raised * share
            weights = exact.astype(bf16)
            out_t = nn(v_t, weights).astype(bf16)
            d_weights = nt(v_, g_)
            delta = jnp.sum(g_t.astype(f32) * out_t.astype(f32), axis=0, keepdims=True)
            d_scores = (exact * (d_weights - delta) * scale).astype(bf16)
            dq_t = nn(k_t, d_scores).astype(bf16)
            d_k += nn(d_scores, q_)
            d_v += nn(weights, g_)
            first = 0 if h == 0 else 5 * HEAD
            pt_n[first:first + HEAD, part] = dq_t[:HEAD]
            out_at = 3 * HEAD - PAD + h * HEAD
            pt_g[out_at:out_at + HEAD, part] = out_t[:HEAD]
            att[part, h * PAD:(h + 1) * PAD] = out_t.T
        first = 0 if h == 0 else 5 * HEAD
        pt_n[first + HEAD:first + 2 * HEAD] = d_k.T[:HEAD].astype(bf16)
        pt_n[first + 2 * HEAD:first + 3 * HEAD] = d_v.T[:HEAD].astype(bf16)

    def chunk(piece, zc, low=0, high=CHUNK):
        block = pl.ds(pl.multiple_of(lax.rem(zc + 2 * nz, nz) * CHUNK + low, 16), high - low)
        n_, g_ = n_t[block], go_t[block]
        if piece == 0:
            a = nn(n_, pn1[...])
            b = nn(g_, pg1[...])
            return jnp.concatenate([a[:, :PAD], a[:, PAD:] + b], axis=1)
        b = nn(g_, pg2[...])
        a = nn(n_, pn2[...])
        return jnp.concatenate([b[:, :PAD], b[:, PAD:] + a[:, :PAD], a[:, PAD:]], axis=1)

    rs_out, rs_in = (rs_out1, rs_out2), (rs_in1, rs_in2)
    x_out, x_in = (x_out1, x_out2), (x_in1, x_in2)
    y_out, y_in = (y_out1, y_out2), (y_in1, y_in2)
    z_sum = (z_sum1, z_sum2)
    rs_copies = {}
    x_copies = {}
    y_copies = {}
    mid = CHUNK // 2
    far = nz // 2

    def rs_send(piece, way, step, part):
        index = (piece * 2 + way) * far + step
        rs_copies[piece, way, step] = send(
            rs_out[piece].at[way, step, part], rs_in[piece].at[way, step, part],
            rs_s.at[index], rs_r.at[index], at_z(z + 1) if way == 0 else at_z(z + nz - 1),
        )

    def rs_first(piece):
        value = chunk(piece, z + far).astype(bf16)
        rs_out[piece][0, 0, :mid] = value[:mid]
        rs_out[piece][1, 0, mid:] = value[mid:]
        rs_send(piece, 0, 0, pl.ds(0, mid))
        rs_send(piece, 1, 0, pl.ds(mid, mid))

    def rs_step(piece, step):
        for way in range(2):
            value = chunk(piece, z + far - step if way == 0 else z - far + step)
            rs_copies[piece, way, step - 1].wait_recv()
            if step == 1:
                if way == 0:
                    got = rs_in[piece][0, 0, :mid].astype(f32)
                    value = jnp.concatenate([value[:mid] + got, value[mid:]], axis=0)
                else:
                    got = rs_in[piece][1, 0, mid:].astype(f32)
                    value = jnp.concatenate([value[:mid], value[mid:] + got], axis=0)
            else:
                value = value + rs_in[piece][way, step - 1].astype(f32)
            rs_out[piece][way, step] = value.astype(bf16)
            rs_send(piece, way, step, pl.ds(0, CHUNK))

    def rs_last(piece):
        value = chunk(piece, z)
        for way in range(2):
            rs_copies[piece, way, far - 1].wait_recv()
            value = value + rs_in[piece][way, far - 1].astype(f32)
        wide = jnp.concatenate([value, jnp.zeros((8, value.shape[1]), f32)], axis=0)
        z_sum[piece][...] = value
        for i in range(NX):
            x_out[piece][i] = wide[i * OWN:i * OWN + SLOT].astype(bf16)
        for k in range(1, NX):
            index = piece * (NX - 1) + k - 1
            x_copies[piece, k] = send(
                x_out[piece].at[lax.rem(x + k, NX)], x_in[piece].at[k - 1],
                x_s.at[index], x_r.at[index], at_x(x + k),
            )

    def x_last(piece):
        value = z_sum[piece][pl.ds(pl.multiple_of(x * OWN, 8), OWN)]
        for k in range(1, NX):
            x_copies[piece, k].wait_recv()
            value = value + x_in[piece][k - 1, :OWN].astype(f32)
        wide = jnp.concatenate([value, jnp.zeros((8, value.shape[1]), f32)], axis=0)
        step = OWN // NS
        for i in range(NS):
            y_out[piece][i] = wide[i * step:i * step + FINAL]
        for k in range(1, NS):
            index = piece * (NS - 1) + k - 1
            y_copies[piece, k] = send(
                y_out[piece].at[lax.rem(s + k, NS)], y_in[piece].at[s],
                y_s.at[index], y_r.at[index], at_s_(s + k),
            )
        y_in[piece][s] = y_out[piece][s]

    head(0)
    pn1[...] = pt_n[:SPLIT].T
    pg1[...] = pt_g[:PAD].T
    rs_first(0)
    head(1)
    at_copies = [
        send(
            att.at[pl.ds(pl.multiple_of(lax.rem(s + k, NS) * ROWS, ROWS), ROWS)], att_all.at[s],
            at_s.at[k - 1], at_r.at[k - 1], at_s_(s + k),
        )
        for k in range(1, NS)
    ]
    att_all[s] = att[mine]
    pg2[...] = pt_g[PAD:].T
    pn2[...] = pt_n[SPLIT + PAD:].T
    rs_first(1)
    rs_step(0, 1)
    rs_step(1, 1)
    for copy in at_copies:
        copy.wait_recv()
    partial_out = nn(att_all[0], wo_pad[:ATT])
    for i in range(1, NS):
        partial_out += nn(att_all[i], wo_pad[i * ATT:(i + 1) * ATT])
    lo_out[...] = partial_out.astype(bf16)
    lo_copy = send(lo_out, lo_in, lo_s, lo_r, other)
    rs_step(0, 2)
    rs_step(1, 2)
    lo_copy.wait_recv()
    both = lo_out[...].astype(f32) + lo_in[...].astype(f32)
    layer_out[:, :HALF] = (pk[0].astype(f32) + both[:, :HALF]).astype(bf16)
    layer_out[:, HALF:] = (pk[1].astype(f32) + both[:, HALF:]).astype(bf16)
    rs_step(0, 3)
    rs_step(1, 3)
    rs_last(0)
    rs_last(1)
    x_last(0)
    x_last(1)
    for piece, lanes in ((0, slice(0, SPLIT)), (1, slice(SPLIT, COLS))):
        for k in range(1, NS):
            y_copies[piece, k].wait_recv()
        grads[:, :, lanes] = y_in[piece][...]
    for copy in started:
        copy.wait_send()


def scratch_shapes(nz):
    far = nz // 2
    w1, w2 = SPLIT, COLS - SPLIT

    def vm(*shape, kind=bf16):
        return pltpu.VMEM(shape, kind)

    def dma(*shape):
        return pltpu.SemaphoreType.DMA(shape)

    return [
        vm(ROWS, HALF), vm(ROWS, HALF), vm(ROWS, HALF), vm(2, ROWS, HALF), vm(2, GROUP, HALF),
        vm(2, GROUP, HALF), vm(D, HALF), vm(D, 6 * PAD), vm(NS * ATT, D), vm(GROUP, 6 * PAD),
        vm(D, GROUP), vm(D, GROUP), vm(GROUP, ATT), vm(ATT, GROUP), vm(GROUP, PAD, kind=f32),
        vm(COLS, GROUP), vm(3 * PAD, GROUP), vm(GROUP, SPLIT), vm(GROUP, PAD), vm(GROUP, 2 * PAD),
        vm(GROUP, 2 * PAD), vm(GROUP, ATT), vm(NS, ROWS, ATT), vm(ROWS, D), vm(ROWS, D),
        vm(2, far, CHUNK, w1), vm(2, far, CHUNK, w1), vm(2, far, CHUNK, w2), vm(2, far, CHUNK, w2),
        vm(NX, SLOT, w1), vm(NX - 1, SLOT, w1), vm(NX, SLOT, w2), vm(NX - 1, SLOT, w2),
        vm(CHUNK, w1, kind=f32), vm(CHUNK, w2, kind=f32),
        vm(NS, FINAL, w1, kind=f32), vm(NS, FINAL, w1, kind=f32),
        vm(NS, FINAL, w2, kind=f32), vm(NS, FINAL, w2, kind=f32),
        dma(12), dma(nz - 1), dma(nz - 1), dma(3), dma(3), dma(3), dma(3), dma(3), dma(3),
        pltpu.SemaphoreType.DMA, pltpu.SemaphoreType.DMA, dma(3), dma(3), dma(3), dma(3),
        dma(3), dma(3), pltpu.SemaphoreType.DMA, pltpu.SemaphoreType.DMA,
        dma(4 * far), dma(4 * far), dma(6), dma(6), dma(6), dma(6),
    ]


def body(patches, arrivals, segment_ids, norm_gain, norm_bias, w_qkv, w_out, grad_out):
    nz = lax.axis_size("dp") // NX
    anywhere = pl.BlockSpec(memory_space=pl.ANY)
    vmem = pl.BlockSpec(memory_space=pltpu.VMEM)
    layer_out, grads = pl.pallas_call(
        functools.partial(kernel, nz),
        out_shape=(
            jax.ShapeDtypeStruct((ROWS, D), bf16),
            jax.ShapeDtypeStruct((NS, FINAL, COLS), f32),
        ),
        in_specs=[anywhere, vmem, vmem, vmem, vmem, anywhere, anywhere, anywhere],
        out_specs=(vmem, vmem),
        scratch_shapes=scratch_shapes(nz),
        compiler_params=pltpu.CompilerParams(
            collective_id=0, has_side_effects=True, vmem_limit_bytes=56 * 1024 * 1024
        ),
    )(
        patches, arrivals, segment_ids.reshape(1, GROUP), norm_gain.reshape(1, D),
        norm_bias.reshape(1, D), w_qkv, w_out, grad_out,
    )
    terms = grads[:, :OWN // NS]
    first, last = 3 * HEAD, 5 * HEAD
    qkv = jnp.concatenate([terms[:, :, :first], terms[:, :, last:]], axis=2)
    qkv = qkv.transpose(1, 0, 2).reshape(OWN // NS, NS * QKV)
    wout = terms[:, :, first:last].transpose(1, 0, 2).reshape(OWN // NS, NS * HEADS_OWN * HEAD)
    return layer_out, qkv, wout


def solution(mesh):
    return jax.shard_map(
        body,
        mesh=mesh,
        in_specs=(
            P(("dp", "seq"), None),
            P(("dp", "seq"), None),
            P("dp"),
            P(),
            P(),
            P(None, "tensor"),
            P("tensor", None),
            P(("dp", "seq"), None),
        ),
        out_specs=(P(("dp", "seq"), None), P(("dp", "seq"), "tensor"), P(("dp", "seq"), "tensor")),
        check_vma=False,
    )
```

```python
import functools

import jax
import jax.numpy as jnp
from jax import lax
from jax.experimental import pallas as pl
from jax.experimental.pallas import tpu as pltpu
from jax.sharding import PartitionSpec as P

HEAD = 80
PAD = 128
HEADS_OWN = 2
NX = 4
NS = 4
ROWS = 128
D = 1280
HALF = D // 2
GROUP = NS * ROWS
QKV = 3 * HEADS_OWN * HEAD
ATT = HEADS_OWN * PAD
COLS = 4 * HEADS_OWN * HEAD
PIECES = ((0, 256), (256, 512), (512, 640))
CHUNK = 160
OWN = 40
FINAL = 16
epsilon = 1e-06
big_negative = -1e30
MESH = pl.DeviceIdType.MESH
bf16 = jnp.bfloat16
f32 = jnp.float32


def nn(a, b):
    return jnp.dot(a, b, preferred_element_type=f32)


def nt(a, b):
    return lax.dot_general(a, b, (((1,), (1,)), ((), ())), preferred_element_type=f32)


def iota(shape, axis):
    return lax.broadcasted_iota(jnp.int32, shape, axis)


def kernel(nz, patches, arrivals, seg, gain, bias, w_qkv, w_out, gout, layer_out, grads, *scratch):
    (az, xs_out, raw, pk, gall, tgt, w_win, w_pad, wo_pad, proj, n_t, go_t, ga, ga_t, segk,
     pt_n, pt_g, pn1, pg1, pg2, pn2, pn3, att, att_all, lo_out, lo_in) = scratch[:26]
    n = len(PIECES)
    rs_out, rs_in = scratch[26:26 + n], scratch[26 + n:26 + 2 * n]
    (fin_out, fin_in, loc, az_s, az_r, gy_s, gy_r, gf_s, gf_r, ax_s, ax_r, tg_s, tg_r, ry_s, ry_r,
     rf_s, rf_r, at_s, at_r, lo_s, lo_r, rs_s, rs_r, fin_s, fin_r) = scratch[26 + 2 * n:]
    dp, s, c = lax.axis_index("dp"), lax.axis_index("seq"), lax.axis_index("tensor")
    z, x = lax.div(dp, NX), lax.rem(dp, NX)
    started = []

    def at_z(zt):
        return {"dp": lax.rem(zt + nz, nz) * NX + x}

    def at_x(xt):
        return {"dp": z * NX + lax.rem(xt + NX, NX)}

    def at_s_(st):
        return {"seq": lax.rem(st + NS, NS)}

    other = {"tensor": 1 - c}

    barrier = pltpu.get_barrier_semaphore()
    far = nz // 2
    partners = (
        [at_z(z + k) for k in sorted(range(1, nz), key=lambda k: abs(k - far))]
        + [at_x(x + k) for k in (2, 1, 3)]
        + [at_s_(s + k) for k in (2, 1, 3)]
        + [other]
    )
    for device in partners:
        pl.semaphore_signal(barrier, inc=1, device_id=device, device_id_type=MESH)

    def send(src, dst, ssem, rsem, device):
        copy = pltpu.make_async_remote_copy(
            src_ref=src, dst_ref=dst, send_sem=ssem, recv_sem=rsem, device_id=device,
            device_id_type=MESH,
        )
        copy.start()
        started.append(copy)
        return copy

    def fetch(src, dst, sem):
        copy = pltpu.make_async_copy(src, dst, sem)
        copy.start()
        return copy

    cols = pl.ds(pl.multiple_of(c * HALF, HALF), HALF)
    mine = pl.ds(pl.multiple_of(s * ROWS, ROWS), ROWS)

    own_patch = fetch(
        patches.at[pl.ds(pl.multiple_of(z * 16, 16), 16), cols],
        az.at[pl.ds(pl.multiple_of(z * 16, 16), 16)], loc.at[0],
    )
    w_start = lax.min(lax.div(QKV * s, 128) * 128, 3 * D // 2 - HALF)
    w_off = QKV * s - w_start
    w_copy = fetch(w_qkv.at[:, pl.ds(pl.multiple_of(w_start, 128), HALF)], w_win, loc.at[3])
    own_gout = [
        fetch(gout.at[:, pl.ds(i * HALF, HALF)], gall.at[i, mine], loc.at[1 + i]) for i in range(2)
    ]
    wo_copies = [
        fetch(w_out.at[pl.ds(i * HEAD, HEAD)], wo_pad.at[pl.ds(i * PAD, HEAD)], loc.at[4 + i])
        for i in range(NS * HEADS_OWN)
    ]
    pl.semaphore_wait(barrier, len(partners))

    az_copies = []
    for k in sorted(range(1, nz), key=lambda k: abs(k - far)):
        zt = lax.rem(z + k, nz)
        az_copies.append(send(
            patches.at[pl.ds(pl.multiple_of(zt * 16, 16), 16), cols],
            az.at[pl.ds(pl.multiple_of(z * 16, 16), 16)],
            az_s.at[k - 1], az_r.at[k - 1], at_z(z + k),
        ))
    gy_copies = {
        k: send(gout.at[:, cols], gall.at[c, mine], gy_s.at[k - 1], gy_r.at[k - 1], at_s_(s + k))
        for k in (1, 3, 2)
    }

    row, col = iota((ROWS, ROWS), 0), iota((ROWS, ROWS), 1)
    to_x = (x + (row >> 5)) & (NX - 1)
    perm = (col == ((row >> 2) & 7) * 16 + to_x * 4 + (row & 3)).astype(bf16)
    slot = iota((32, ROWS), 1)
    origin = ((slot >> 2) & 7) * NX + ((x + (slot >> 5)) & (NX - 1))
    counter = iota((32, ROWS), 0)
    counts = jnp.broadcast_to(arrivals[...].astype(f32), (16, 32)).astype(bf16)
    starts = nn(counts, (counter < origin).astype(bf16))[0:8]
    number = nn(counts, (counter == origin).astype(bf16))[0:8]
    place = (iota((8, ROWS), 1) & 3).astype(f32)
    tgt[s] = jnp.where(place < number, starts + place, -1.0)
    tg_copies = {
        k: send(tgt.at[s], tgt.at[s], tg_s.at[k - 1], tg_r.at[k - 1], at_s_(s + k))
        for k in (1, 3, 2)
    }

    ids = seg[...].astype(f32)
    key_ids = jnp.where(ids < 0.0, -2.0, ids)
    segk[...] = jnp.broadcast_to(key_ids, (PAD, GROUP)).T

    for i in range(NS * HEADS_OWN):
        wo_pad[i * PAD + HEAD:(i + 1) * PAD] = jnp.zeros((PAD - HEAD, D), bf16)
    pt_n[3 * HEAD:5 * HEAD] = jnp.zeros((2 * HEAD, GROUP), bf16)
    pt_g[...] = jnp.zeros(pt_g.shape, bf16)

    w_copy.wait()

    def pad_pair(i, carry):
        r, cc = iota((HALF, 2 * PAD), 0), iota((HALF, 2 * PAD), 1)
        d = cc & (PAD - 1)
        wanted = w_off + (2 * i + (cc >> 7)) * HEAD + d
        chosen = ((r == wanted) & (d < HEAD)).astype(bf16)
        out = pl.ds(pl.multiple_of(i * 2 * PAD, 2 * PAD), 2 * PAD)
        w_pad[:, out] = nn(w_win[...], chosen).astype(bf16)
        return carry

    lax.fori_loop(0, 3, pad_pair, 0)

    own_patch.wait()
    for copy in az_copies:
        copy.wait_recv()
    xs = nn(perm, az[...]).astype(bf16)
    quarter = ROWS // NX
    xs_out[...] = xs
    raw[c, pl.ds(pl.multiple_of(s * ROWS, ROWS), quarter)] = xs[:quarter]
    ax_copies = []
    for k in (1, 3, 2):
        landing = pl.multiple_of(s * ROWS + (NX - k) * quarter, quarter)
        ax_copies.append(send(
            xs_out.at[pl.ds(k * quarter, quarter)], raw.at[c, pl.ds(landing, quarter)],
            ax_s.at[k - 1], ax_r.at[k - 1], at_x(x + k),
        ))
    first = pl.ds(pl.multiple_of(s * ROWS, ROWS), quarter)
    rest = pl.ds(pl.multiple_of(s * ROWS + quarter, quarter), ROWS - quarter)
    ry_copies, rf_copies = {}, {}

    def spread(part, block):
        for k in (1, 3, 2):
            ry_copies[part, k] = send(
                raw.at[c, block], raw.at[c, block], ry_s.at[3 * part + k - 1],
                ry_r.at[3 * part + k - 1], at_s_(s + k),
            )
        rf_copies[part] = send(
            raw.at[c, block], raw.at[c, block], rf_s.at[part], rf_r.at[part], other
        )

    spread(0, first)
    for copy in ax_copies:
        copy.wait_recv()
    spread(1, rest)

    def peer(k):
        return lax.rem(s + NS - k, NS)

    def rows_of(index):
        return pl.ds(pl.multiple_of(index * ROWS, ROWS), ROWS)

    def take(index):
        block = rows_of(index)
        pick = (row.astype(f32) == tgt[index][0:1]).astype(bf16)
        x0, x1 = nn(pick, raw[0, block]), nn(pick, raw[1, block])
        y0, y1 = x0, x1
        mean = (jnp.sum(x0, axis=1, keepdims=True) + jnp.sum(x1, axis=1, keepdims=True)) / D
        x0, x1 = x0 - mean, x1 - mean
        var = (jnp.sum(x0 * x0, axis=1, keepdims=True) + jnp.sum(x1 * x1, axis=1, keepdims=True)) / D
        inv = lax.rsqrt(var + epsilon)
        gains, biases = gain[...].reshape(1, D), bias[...].reshape(1, D)
        x0 = (x0 * inv * gains[:, :HALF] + biases[:, :HALF]).astype(bf16)
        x1 = (x1 * inv * gains[:, HALF:] + biases[:, HALF:]).astype(bf16)
        proj[block] = (nn(x0, w_pad[:HALF]) + nn(x1, w_pad[HALF:])).astype(bf16)
        n_t[:HALF, block] = x0.T
        n_t[HALF:, block] = x1.T
        return y0, y1

    gf_copies = []
    for k in (1, 3, 2):
        gy_copies[k].wait_recv()
        block = rows_of(peer(k))
        gf_copies.append(send(
            gall.at[c, block], gall.at[c, block], gf_s.at[k - 1], gf_r.at[k - 1], other
        ))
    for part in range(2):
        rf_copies[part].wait_recv()
    own0, own1 = take(s)
    pk[0] = own0.astype(bf16)
    pk[1] = own1.astype(bf16)
    for copy in wo_copies:
        copy.wait()
    for copy in own_gout:
        copy.wait()
    for copy in gf_copies:
        copy.wait_recv()
    wo_mine = wo_pad[pl.ds(pl.multiple_of(s * ATT, ATT), ATT)]
    ga[...] = (nt(gall[0], wo_mine[:, :HALF]) + nt(gall[1], wo_mine[:, HALF:])).astype(bf16)
    ga_t[...] = (nt(wo_mine[:, :HALF], gall[0]) + nt(wo_mine[:, HALF:], gall[1])).astype(bf16)
    go_t[:HALF] = gall[0].T
    go_t[HALF:] = gall[1].T

    def pass_on(k):
        for part in range(2):
            ry_copies[part, k].wait_recv()
        tg_copies[k].wait_recv()
        block = rows_of(peer(k))
        rf_copies[1 + k] = send(
            raw.at[c, block], raw.at[c, block], rf_s.at[1 + k], rf_r.at[1 + k], other
        )

    def take_peer(k):
        rf_copies[1 + k].wait_recv()
        take(peer(k))

    pass_on(1)
    pass_on(3)
    take_peer(1)
    take_peer(3)
    pass_on(2)
    take_peer(2)

    scale = HEAD ** (-0.5)
    to_exp2 = scale * 1.4426950408889634
    query_ids = ids

    def head(h):
        base = 3 * PAD * h
        k_, v_ = proj[:, base + PAD:base + 2 * PAD], proj[:, base + 2 * PAD:base + 3 * PAD]
        k_t, v_t = k_.T, v_.T
        d_k = jnp.zeros((GROUP, PAD), f32)
        d_v = jnp.zeros((GROUP, PAD), f32)
        wide = 256
        for b in range(GROUP // wide):
            part = slice(b * wide, (b + 1) * wide)
            q_ = proj[part, base:base + PAD]
            g_ = ga[part, h * PAD:(h + 1) * PAD]
            g_t = ga_t[h * PAD:(h + 1) * PAD, part]
            scores = nt(k_, q_)
            keys = jnp.concatenate([segk[...]] * (wide // PAD), axis=1)
            masked = jnp.where(keys == query_ids[:, part], scores, big_negative)
            top = jnp.max(masked, axis=0, keepdims=True)
            raised = jnp.exp2((masked - top) * to_exp2)
            total = jnp.sum(raised, axis=0, keepdims=True)
            share = jnp.where(query_ids[:, part] < 0.0, 0.0, 1.0 / total)
            exact = raised * share
            weights = exact.astype(bf16)
            out_t = nn(v_t, weights).astype(bf16)
            d_weights = nt(v_, g_)
            delta = jnp.sum(g_t.astype(f32) * out_t.astype(f32), axis=0, keepdims=True)
            d_scores = (exact * (d_weights - delta) * scale).astype(bf16)
            dq_t = nn(k_t, d_scores).astype(bf16)
            d_k += nn(d_scores, q_)
            d_v += nn(weights, g_)
            start = 0 if h == 0 else 5 * HEAD
            pt_n[start:start + HEAD, part] = dq_t[:HEAD]
            out_at = 3 * HEAD - PAD + h * HEAD
            pt_g[out_at:out_at + HEAD, part] = out_t[:HEAD]
            att[part, h * PAD:(h + 1) * PAD] = out_t.T
        start = 0 if h == 0 else 5 * HEAD
        pt_n[start + HEAD:start + 2 * HEAD] = d_k.T[:HEAD].astype(bf16)
        pt_n[start + 2 * HEAD:start + 3 * HEAD] = d_v.T[:HEAD].astype(bf16)

    def chunk(piece, zc):
        block = pl.ds(pl.multiple_of(lax.rem(zc + 2 * nz, nz) * CHUNK, 16), CHUNK)
        if piece == 0:
            a = nn(n_t[block], pn1[...])
            b = nn(go_t[block], pg1[...])
            return jnp.concatenate([a[:, :PAD], a[:, PAD:] + b], axis=1)
        if piece == 1:
            b = nn(go_t[block], pg2[...])
            a = nn(n_t[block], pn2[...])
            return jnp.concatenate([b[:, :PAD], b[:, PAD:] + a], axis=1)
        return nn(n_t[block], pn3[...])

    rs_copies = {}
    mid = CHUNK // 2

    def rs_send(piece, way, step, part):
        index = (piece * 2 + way) * far + step
        rs_copies[piece, way, step] = send(
            rs_out[piece].at[way, step, part], rs_in[piece].at[way, step, part],
            rs_s.at[index], rs_r.at[index], at_z(z + 1) if way == 0 else at_z(z + nz - 1),
        )

    def rs_first(piece):
        value = chunk(piece, z + far).astype(bf16)
        rs_out[piece][0, 0, :mid] = value[:mid]
        rs_out[piece][1, 0, mid:] = value[mid:]
        rs_send(piece, 0, 0, pl.ds(0, mid))
        rs_send(piece, 1, 0, pl.ds(mid, mid))

    def rs_step(piece, step):
        for way in range(2):
            value = chunk(piece, z + far - step if way == 0 else z - far + step)
            rs_copies[piece, way, step - 1].wait_recv()
            if step == 1:
                if way == 0:
                    got = rs_in[piece][0, 0, :mid].astype(f32)
                    value = jnp.concatenate([value[:mid] + got, value[mid:]], axis=0)
                else:
                    got = rs_in[piece][1, 0, mid:].astype(f32)
                    value = jnp.concatenate([value[:mid], value[mid:] + got], axis=0)
            else:
                value = value + rs_in[piece][way, step - 1].astype(f32)
            rs_out[piece][way, step] = value.astype(bf16)
            rs_send(piece, way, step, pl.ds(0, CHUNK))

    per = OWN // NS

    def rs_last(piece):
        value = chunk(piece, z)
        for way in range(2):
            rs_copies[piece, way, far - 1].wait_recv()
            value = value + rs_in[piece][way, far - 1].astype(f32)
        wide = jnp.concatenate([value, jnp.zeros((8, value.shape[1]), f32)], axis=0)
        for i in range(NX * NS):
            fin_out[i, :, PIECES[piece][0]:PIECES[piece][1]] = wide[i * per:i * per + FINAL].astype(bf16)

    fin_copies = {}
    fin_lanes = ((0, 512), (512, 640))

    def fin_send(part):
        low, high = fin_lanes[part]
        for kx in (2, 1, 3, 0):
            for ks in (2, 1, 3, 0):
                if kx or ks:
                    index = NS * kx + ks
                    to = lax.rem(x + kx, NX) * NS + lax.rem(s + ks, NS)
                    device = {"dp": z * NX + lax.rem(x + kx, NX), "seq": lax.rem(s + ks, NS)}
                    fin_copies[part, index] = send(
                        fin_out.at[to, :, pl.ds(low, high - low)],
                        fin_in.at[index, :, pl.ds(low, high - low)],
                        fin_s.at[part * NX * NS + index], fin_r.at[part * NX * NS + index], device,
                    )

    def fin_sum(part):
        low, high = fin_lanes[part]
        for ks in (1, 3, 2, 0):
            total = None
            for kx in range(NX):
                if kx or ks:
                    fin_copies[part, NS * kx + ks].wait_recv()
                    term = fin_in[NS * kx + ks, :, low:high].astype(f32)
                else:
                    term = fin_out[x * NS + s, :, low:high].astype(f32)
                total = term if total is None else total + term
            grads[lax.rem(s + NS - ks, NS), :, low:high] = total

    head(0)
    pn1[...] = pt_n[:256].T
    pg1[...] = pt_g[:PAD].T
    rs_first(0)
    head(1)
    pg2[...] = pt_g[PAD:].T
    pn2[...] = pt_n[3 * PAD:4 * PAD].T
    rs_first(1)
    pn3[...] = pt_n[4 * PAD:].T
    rs_first(2)
    at_copies = [
        send(
            att.at[rows_of(lax.rem(s + k, NS))], att_all.at[s],
            at_s.at[k - 1], at_r.at[k - 1], at_s_(s + k),
        )
        for k in range(1, NS)
    ]
    att_all[s] = att[mine]
    for piece in range(n):
        rs_step(piece, 1)
    for copy in at_copies:
        copy.wait_recv()
    partial_out = nn(att_all[0], wo_pad[:ATT])
    for i in range(1, NS):
        partial_out += nn(att_all[i], wo_pad[i * ATT:(i + 1) * ATT])
    lo_out[...] = partial_out.astype(bf16)
    lo_copy = send(lo_out, lo_in, lo_s, lo_r, other)
    for piece in range(n):
        rs_step(piece, 2)
    lo_copy.wait_recv()
    both = lo_out[...].astype(f32) + lo_in[...].astype(f32)
    layer_out[:, :HALF] = (pk[0].astype(f32) + both[:, :HALF]).astype(bf16)
    layer_out[:, HALF:] = (pk[1].astype(f32) + both[:, HALF:]).astype(bf16)
    for piece in range(n):
        rs_step(piece, 3)
    rs_last(0)
    rs_last(1)
    fin_send(0)
    rs_last(2)
    fin_send(1)
    fin_sum(0)
    fin_sum(1)
    for copy in started:
        copy.wait_send()


def finish(layer_in, grads, layer_out, qkv, wout):
    per, first, last = OWN // NS, 3 * HEAD, 5 * HEAD
    layer_out[...] = layer_in[...]
    blocks = [grads[i][:per] for i in range(NS)]
    spans = ((0, first), (last, COLS))
    qkv[...] = jnp.concatenate([b[:, low:high] for b in blocks for low, high in spans], axis=1)
    wout[...] = jnp.concatenate([b[:, first:last] for b in blocks], axis=1)


def scratch_shapes(nz):
    far = nz // 2

    def vm(*shape, kind=bf16):
        return pltpu.VMEM(shape, kind)

    def dma(*shape):
        return pltpu.SemaphoreType.DMA(shape)

    one = pltpu.SemaphoreType.DMA
    rings = [vm(2, far, CHUNK, high - low) for low, high in PIECES]
    return [
        vm(ROWS, HALF), vm(ROWS, HALF), vm(2, GROUP, HALF), vm(2, ROWS, HALF), vm(2, GROUP, HALF),
        vm(NS, 8, ROWS, kind=f32), vm(D, HALF), vm(D, 6 * PAD), vm(NS * ATT, D),
        vm(GROUP, 6 * PAD), vm(D, GROUP), vm(D, GROUP), vm(GROUP, ATT), vm(ATT, GROUP),
        vm(GROUP, PAD, kind=f32), vm(COLS, GROUP), vm(3 * PAD, GROUP), vm(GROUP, 2 * PAD),
        vm(GROUP, PAD), vm(GROUP, 2 * PAD), vm(GROUP, PAD), vm(GROUP, PAD), vm(GROUP, ATT),
        vm(NS, ROWS, ATT), vm(ROWS, D), vm(ROWS, D),
        *rings, *rings, vm(NX * NS, FINAL, COLS), vm(NX * NS, FINAL, COLS),
        dma(12), dma(nz - 1), dma(nz - 1), dma(3), dma(3), dma(3), dma(3), dma(3), dma(3),
        dma(3), dma(3), dma(6), dma(6), dma(5), dma(5), dma(3), dma(3), one, one,
        dma(2 * len(PIECES) * far), dma(2 * len(PIECES) * far),
        dma(2 * NX * NS), dma(2 * NX * NS),
    ]


def body(patches, arrivals, segment_ids, norm_gain, norm_bias, w_qkv, w_out, grad_out):
    nz = lax.axis_size("dp") // NX
    anywhere = pl.BlockSpec(memory_space=pl.ANY)
    vmem = pl.BlockSpec(memory_space=pltpu.VMEM)
    layer, grads = pl.pallas_call(
        functools.partial(kernel, nz),
        out_shape=(
            jax.ShapeDtypeStruct((ROWS, D), bf16),
            jax.ShapeDtypeStruct((NS, FINAL, COLS), f32),
        ),
        in_specs=[anywhere, vmem, vmem, vmem, vmem, anywhere, anywhere, anywhere],
        out_specs=(vmem, vmem),
        scratch_shapes=scratch_shapes(nz),
        compiler_params=pltpu.CompilerParams(
            collective_id=0, has_side_effects=True, vmem_limit_bytes=56 * 1024 * 1024
        ),
    )(
        patches, arrivals, segment_ids.reshape(1, GROUP), norm_gain, norm_bias, w_qkv, w_out,
        grad_out,
    )
    per = OWN // NS
    return pl.pallas_call(
        finish,
        out_shape=(
            jax.ShapeDtypeStruct((ROWS, D), bf16),
            jax.ShapeDtypeStruct((per, NS * QKV), f32),
            jax.ShapeDtypeStruct((per, NS * HEADS_OWN * HEAD), f32),
        ),
        in_specs=[vmem, vmem],
        out_specs=(vmem, vmem, vmem),
    )(layer, grads)


def solution(mesh):
    return jax.shard_map(
        body,
        mesh=mesh,
        in_specs=(
            P(("dp", "seq"), None),
            P(("dp", "seq"), None),
            P("dp"),
            P(),
            P(),
            P(None, "tensor"),
            P("tensor", None),
            P(("dp", "seq"), None),
        ),
        out_specs=(P(("dp", "seq"), None), P(("dp", "seq"), "tensor"), P(("dp", "seq"), "tensor")),
        check_vma=False,
    )
```

```python
import functools

import jax
import jax.numpy as jnp
from jax import lax
from jax.experimental import pallas as pl
from jax.experimental.pallas import tpu as pltpu
from jax.sharding import PartitionSpec as P

HEAD = 80
PAD = 128
HEADS_OWN = 2
NX = 4
NS = 4
ROWS = 128
D = 1280
HALF = D // 2
GROUP = NS * ROWS
QKV = 3 * HEADS_OWN * HEAD
ATT = HEADS_OWN * PAD
COLS = 4 * HEADS_OWN * HEAD
PIECES = ((0, 256), (256, 512), (512, 640))
CHUNK = 160
OWN = 40
FINAL = 16
epsilon = 1e-06
big_negative = -1e30
MESH = pl.DeviceIdType.MESH
bf16 = jnp.bfloat16
remote = pltpu.make_async_remote_copy
f32 = jnp.float32


def nn(a, b):
    return jnp.dot(a, b, preferred_element_type=f32)


def nt(a, b):
    return lax.dot_general(a, b, (((1,), (1,)), ((), ())), preferred_element_type=f32)


def iota(shape, axis):
    return lax.broadcasted_iota(jnp.int32, shape, axis)


def kernel(nz, patches, arrivals, seg, gain, bias, w_qkv, w_out, gout, layer_out, grads, *scratch):
    (arrivals_v, seg_v, gain_v, bias_v,
     az, xs_out, raw, pk, gall, tgt, w_win, w_pad, wo_pad, proj, n_t, go_t, ga, ga_t, segk,
     pt_n, pt_g, pn1, pg1, pg2, pn2, pn3, att, att_all, lo_out, lo_in) = scratch[:30]
    n = len(PIECES)
    rs_out, rs_in = scratch[30:30 + n], scratch[30 + n:30 + 2 * n]
    (fin_out, fin_in, ready, loc, az_s, az_r, gy_s, gy_r, gf_s, gf_r, ax_s, ax_r, ow_s, ow_r,
     tg_s, tg_r, ry_s, ry_r,
     rf_s, rf_r, at_s, at_r, lo_s, lo_r, rs_s, rs_r, fin_s, fin_r) = scratch[30 + 2 * n:]
    dp, s, c = lax.axis_index("dp"), lax.axis_index("seq"), lax.axis_index("tensor")
    z, x = lax.div(dp, NX), lax.rem(dp, NX)
    started = []

    def at_z(zt):
        return {"dp": lax.rem(zt + nz, nz) * NX + x}

    def at_x(xt):
        return {"dp": z * NX + lax.rem(xt + NX, NX)}

    def at_s_(st):
        return {"seq": lax.rem(st + NS, NS)}

    other = {"tensor": 1 - c}

    barrier = pltpu.get_barrier_semaphore()
    far = nz // 2
    ways_z = sorted(range(1, nz), key=lambda k: abs(k - far))
    partners = (
        [at_z(z + k) for k in ways_z]
        + [at_x(x + k) for k in (2, 1, 3)]
        + [at_s_(s + k) for k in (2, 1, 3)]
    )
    across = [other] + [dict(at_x(x + k), tensor=1 - c) for k in (2, 1, 3)]
    for device in partners:
        pl.semaphore_signal(barrier, inc=1, device_id=device, device_id_type=MESH)

    @pl.when(c == 0)
    def _():
        for device in across:
            pl.semaphore_signal(barrier, inc=1, device_id=device, device_id_type=MESH)

    def send(src, dst, ssem, rsem, device):
        copy = pltpu.make_async_remote_copy(
            src_ref=src, dst_ref=dst, send_sem=ssem, recv_sem=rsem, device_id=device,
            device_id_type=MESH,
        )
        copy.start()
        started.append(copy)
        return copy

    def fetch(src, dst, sem):
        copy = pltpu.make_async_copy(src, dst, sem)
        copy.start()
        return copy

    cols = pl.ds(pl.multiple_of(c * HALF, HALF), HALF)
    mine = pl.ds(pl.multiple_of(s * ROWS, ROWS), ROWS)

    own_patch = fetch(
        patches.at[pl.ds(pl.multiple_of(z * 16, 16), 16)],
        az.at[pl.ds(pl.multiple_of(z * 16, 16), 16)], loc.at[0],
    )
    small = [
        fetch(a, b, loc.at[12 + i])
        for i, (a, b) in enumerate(
            ((arrivals, arrivals_v), (seg, seg_v), (gain, gain_v), (bias, bias_v))
        )
    ]
    w_start = lax.min(lax.div(QKV * s, 128) * 128, 3 * D // 2 - HALF)
    w_off = QKV * s - w_start
    w_copy = fetch(w_qkv.at[:, pl.ds(pl.multiple_of(w_start, 128), HALF)], w_win, loc.at[3])
    own_gout = [
        fetch(gout.at[:, pl.ds(i * HALF, HALF)], gall.at[i, mine], loc.at[1 + i]) for i in range(2)
    ]
    wo_copies = [
        fetch(w_out.at[pl.ds(i * HEAD, HEAD)], wo_pad.at[pl.ds(i * PAD, HEAD)], loc.at[4 + i])
        for i in range(NS * HEADS_OWN)
    ]
    az_copies = []
    for k in ways_z:
        zt = lax.rem(z + k, nz)
        az_copies.append(remote(
            src_ref=patches.at[pl.ds(pl.multiple_of(zt * 16, 16), 16)],
            dst_ref=az.at[pl.ds(pl.multiple_of(z * 16, 16), 16)],
            send_sem=az_s.at[k - 1], recv_sem=az_r.at[k - 1], device_id=at_z(z + k),
            device_id_type=MESH,
        ))

    @pl.when(c == 0)
    def _():
        pl.semaphore_wait(barrier, len(partners))
        for copy in az_copies:
            copy.start()

    @pl.when(c == 1)
    def _():
        pl.semaphore_wait(barrier, len(partners) + len(across))
        for device in across:
            pl.semaphore_signal(ready, inc=1, device_id=device, device_id_type=MESH)

    gy_copies = {
        k: send(gout.at[:, cols], gall.at[c, mine], gy_s.at[k - 1], gy_r.at[k - 1], at_s_(s + k))
        for k in (1, 3, 2)
    }

    for copy in small:
        copy.wait()

    row, col = iota((ROWS, ROWS), 0), iota((ROWS, ROWS), 1)
    to_x = (x + (row >> 5)) & (NX - 1)
    perm = (col == ((row >> 2) & 7) * 16 + to_x * 4 + (row & 3)).astype(bf16)
    slot = iota((32, ROWS), 1)
    spot = slot >> 5
    step = jnp.where(spot == 1, 3, jnp.where(spot > 1, spot - 1, 0))
    origin = ((slot >> 2) & 7) * NX + ((x + step) & (NX - 1))
    counter = iota((32, ROWS), 0)
    counts = jnp.broadcast_to(arrivals_v[...].astype(f32), (16, 32)).astype(bf16)
    starts = nn(counts, (counter < origin).astype(bf16))[0:8]
    number = nn(counts, (counter == origin).astype(bf16))[0:8]
    place = (iota((8, ROWS), 1) & 3).astype(f32)
    tgt[s] = jnp.where(place < number, starts + place, -1.0)
    tg_copies = {
        k: send(tgt.at[s], tgt.at[s], tg_s.at[k - 1], tg_r.at[k - 1], at_s_(s + k))
        for k in (1, 3, 2)
    }

    ids = seg_v[...].astype(f32)
    key_ids = jnp.where(ids < 0.0, -2.0, ids)
    segk[...] = jnp.broadcast_to(key_ids, (PAD, GROUP)).T

    for i in range(NS * HEADS_OWN):
        wo_pad[i * PAD + HEAD:(i + 1) * PAD] = jnp.zeros((PAD - HEAD, D), bf16)
    pt_n[3 * HEAD:5 * HEAD] = jnp.zeros((2 * HEAD, GROUP), bf16)
    pt_g[...] = jnp.zeros(pt_g.shape, bf16)

    w_copy.wait()

    def pad_pair(i, carry):
        r, cc = iota((HALF, 2 * PAD), 0), iota((HALF, 2 * PAD), 1)
        d = cc & (PAD - 1)
        wanted = w_off + (2 * i + (cc >> 7)) * HEAD + d
        chosen = ((r == wanted) & (d < HEAD)).astype(bf16)
        out = pl.ds(pl.multiple_of(i * 2 * PAD, 2 * PAD), 2 * PAD)
        w_pad[:, out] = nn(w_win[...], chosen).astype(bf16)
        return carry

    lax.fori_loop(0, 3, pad_pair, 0)

    quarter = ROWS // NX
    first = pl.ds(pl.multiple_of(s * ROWS, ROWS), quarter)
    spots = {1: 1, 3: 2, 2: 3}

    def landing(k):
        return pl.ds(pl.multiple_of(s * ROWS + spots[k] * quarter, quarter), quarter)

    ax_copies = {
        (h, k): remote(
            src_ref=xs_out.at[pl.ds(k * quarter, quarter), pl.ds(h * HALF, HALF)],
            dst_ref=raw.at[h, landing(k)],
            send_sem=ax_s.at[3 * h + k - 1], recv_sem=ax_r.at[k - 1],
            device_id=dict(at_x(x + k), tensor=h), device_id_type=MESH,
        )
        for h in range(2) for k in (1, 3, 2)
    }
    own_half = remote(
        src_ref=xs_out.at[pl.ds(0, quarter), pl.ds(HALF, HALF)], dst_ref=raw.at[1, first],
        send_sem=ow_s, recv_sem=ow_r, device_id=other, device_id_type=MESH,
    )

    @pl.when(c == 0)
    def _():
        own_patch.wait()
        for copy in az_copies:
            copy.wait_recv()
        xs = nn(perm, az[...]).astype(bf16)
        xs_out[...] = xs
        raw[0, first] = xs[:quarter, :HALF]
        pl.semaphore_wait(ready, len(across))
        for k in (1, 3, 2):
            for h in range(2):
                ax_copies[h, k].start()
        own_half.start()

    @pl.when(c == 1)
    def _():
        own_patch.wait()
        own_half.wait_recv()

    ry_copies, rf_copies = {}, {}

    def spread(part, block):
        for k in (1, 3, 2):
            ry_copies[part, k] = send(
                raw.at[c, block], raw.at[c, block], ry_s.at[3 * part + k - 1],
                ry_r.at[3 * part + k - 1], at_s_(s + k),
            )
        rf_copies[part] = send(
            raw.at[c, block], raw.at[c, block], rf_s.at[part], rf_r.at[part], other
        )

    spread(0, first)
    ax_copies[0, 1].wait_recv()
    ax_copies[0, 3].wait_recv()
    spread(1, pl.ds(pl.multiple_of(s * ROWS + quarter, quarter), 2 * quarter))
    ax_copies[0, 2].wait_recv()
    spread(2, landing(2))

    def peer(k):
        return lax.rem(s + NS - k, NS)

    def rows_of(index):
        return pl.ds(pl.multiple_of(index * ROWS, ROWS), ROWS)

    def take(index):
        block = rows_of(index)
        pick = (row.astype(f32) == tgt[index][0:1]).astype(bf16)
        x0, x1 = nn(pick, raw[0, block]), nn(pick, raw[1, block])
        y0, y1 = x0, x1
        mean = (jnp.sum(x0, axis=1, keepdims=True) + jnp.sum(x1, axis=1, keepdims=True)) / D
        x0, x1 = x0 - mean, x1 - mean
        var = (jnp.sum(x0 * x0, axis=1, keepdims=True) + jnp.sum(x1 * x1, axis=1, keepdims=True)) / D
        inv = lax.rsqrt(var + epsilon)
        gains, biases = gain_v[...].reshape(1, D), bias_v[...].reshape(1, D)
        x0 = (x0 * inv * gains[:, :HALF] + biases[:, :HALF]).astype(bf16)
        x1 = (x1 * inv * gains[:, HALF:] + biases[:, HALF:]).astype(bf16)
        proj[block] = (nn(x0, w_pad[:HALF]) + nn(x1, w_pad[HALF:])).astype(bf16)
        n_t[:HALF, block] = x0.T
        n_t[HALF:, block] = x1.T
        return y0, y1

    gf_copies = []
    for k in (1, 3, 2):
        gy_copies[k].wait_recv()
        block = rows_of(peer(k))
        gf_copies.append(send(
            gall.at[c, block], gall.at[c, block], gf_s.at[k - 1], gf_r.at[k - 1], other
        ))
    for part in range(3):
        rf_copies[part].wait_recv()
    own0, own1 = take(s)
    pk[0] = own0.astype(bf16)
    pk[1] = own1.astype(bf16)
    for copy in wo_copies:
        copy.wait()
    for copy in own_gout:
        copy.wait()
    for copy in gf_copies:
        copy.wait_recv()
    wo_mine = wo_pad[pl.ds(pl.multiple_of(s * ATT, ATT), ATT)]
    ga[...] = (nt(gall[0], wo_mine[:, :HALF]) + nt(gall[1], wo_mine[:, HALF:])).astype(bf16)
    ga_t[...] = (nt(wo_mine[:, :HALF], gall[0]) + nt(wo_mine[:, HALF:], gall[1])).astype(bf16)
    go_t[:HALF] = gall[0].T
    go_t[HALF:] = gall[1].T

    def pass_on(k):
        for part in range(3):
            ry_copies[part, k].wait_recv()
        tg_copies[k].wait_recv()
        block = rows_of(peer(k))
        rf_copies[2 + k] = send(
            raw.at[c, block], raw.at[c, block], rf_s.at[2 + k], rf_r.at[2 + k], other
        )

    def take_peer(k):
        rf_copies[2 + k].wait_recv()
        take(peer(k))

    pass_on(1)
    pass_on(3)
    take_peer(1)
    take_peer(3)
    pass_on(2)
    take_peer(2)

    @pl.when(c == 0)
    def _():
        for copy in az_copies + list(ax_copies.values()) + [own_half]:
            copy.wait_send()

    scale = HEAD ** (-0.5)
    to_exp2 = scale * 1.4426950408889634
    query_ids = ids

    def head(h):
        base = 3 * PAD * h
        k_, v_ = proj[:, base + PAD:base + 2 * PAD], proj[:, base + 2 * PAD:base + 3 * PAD]
        k_t, v_t = k_.T, v_.T
        wide = 256
        parts = [slice(b * wide, (b + 1) * wide) for b in range(GROUP // wide)]
        keys = jnp.concatenate([segk[...]] * (wide // PAD), axis=1)
        q_ = [proj[part, base:base + PAD] for part in parts]
        g_ = [ga[part, h * PAD:(h + 1) * PAD] for part in parts]
        scores = [nt(k_, q) for q in q_]
        d_weights = [nt(v_, g) for g in g_]
        raised, share = [], []
        for part, score in zip(parts, scores):
            masked = jnp.where(keys == query_ids[:, part], score, big_negative)
            top = jnp.max(masked, axis=0, keepdims=True)
            up = jnp.exp2((masked - top) * to_exp2)
            total = jnp.sum(up, axis=0, keepdims=True)
            raised.append(up)
            share.append(jnp.where(query_ids[:, part] < 0.0, 0.0, 1.0 / total))
        d_k = d_v = None
        start = 0 if h == 0 else 5 * HEAD
        out_at = 3 * HEAD - PAD + h * HEAD
        for part, q, g, up, sh, dw in zip(parts, q_, g_, raised, share, d_weights):
            g_t = ga_t[h * PAD:(h + 1) * PAD, part]
            exact = up * sh
            weights = exact.astype(bf16)
            out_t = nn(v_t, weights).astype(bf16)
            term = nn(weights, g)
            d_v = term if d_v is None else d_v + term
            delta = jnp.sum(g_t.astype(f32) * out_t.astype(f32), axis=0, keepdims=True)
            d_scores = (exact * (dw - delta) * scale).astype(bf16)
            dq_t = nn(k_t, d_scores).astype(bf16)
            term = nn(d_scores, q)
            d_k = term if d_k is None else d_k + term
            pt_n[start:start + HEAD, part] = dq_t[:HEAD]
            pt_g[out_at:out_at + HEAD, part] = out_t[:HEAD]
            att[part, h * PAD:(h + 1) * PAD] = out_t.T
        pt_n[start + HEAD:start + 2 * HEAD] = d_k.T[:HEAD].astype(bf16)
        pt_n[start + 2 * HEAD:start + 3 * HEAD] = d_v.T[:HEAD].astype(bf16)

    def chunk(piece, zc):
        block = pl.ds(pl.multiple_of(lax.rem(zc + 2 * nz, nz) * CHUNK, 16), CHUNK)
        if piece == 0:
            a = nn(n_t[block], pn1[...])
            b = nn(go_t[block], pg1[...])
            return jnp.concatenate([a[:, :PAD], a[:, PAD:] + b], axis=1)
        if piece == 1:
            b = nn(go_t[block], pg2[...])
            a = nn(n_t[block], pn2[...])
            return jnp.concatenate([b[:, :PAD], b[:, PAD:] + a], axis=1)
        return nn(n_t[block], pn3[...])

    rs_copies = {}
    mid = CHUNK // 2

    def rs_send(piece, way, step, part):
        index = (piece * 2 + way) * far + step
        rs_copies[piece, way, step] = send(
            rs_out[piece].at[way, step, part], rs_in[piece].at[way, step, part],
            rs_s.at[index], rs_r.at[index], at_z(z + 1) if way == 0 else at_z(z + nz - 1),
        )

    def rs_first(piece):
        value = chunk(piece, z + far).astype(bf16)
        rs_out[piece][0, 0, :mid] = value[:mid]
        rs_out[piece][1, 0, mid:] = value[mid:]
        rs_send(piece, 0, 0, pl.ds(0, mid))
        rs_send(piece, 1, 0, pl.ds(mid, mid))

    def rs_step(piece, step):
        for way in range(2):
            value = chunk(piece, z + far - step if way == 0 else z - far + step)
            rs_copies[piece, way, step - 1].wait_recv()
            if step == 1:
                if way == 0:
                    got = rs_in[piece][0, 0, :mid].astype(f32)
                    value = jnp.concatenate([value[:mid] + got, value[mid:]], axis=0)
                else:
                    got = rs_in[piece][1, 0, mid:].astype(f32)
                    value = jnp.concatenate([value[:mid], value[mid:] + got], axis=0)
            else:
                value = value + rs_in[piece][way, step - 1].astype(f32)
            rs_out[piece][way, step] = value.astype(bf16)
            rs_send(piece, way, step, pl.ds(0, CHUNK))

    per = OWN // NS

    def rs_last(piece):
        value = chunk(piece, z)
        for way in range(2):
            rs_copies[piece, way, far - 1].wait_recv()
            value = value + rs_in[piece][way, far - 1].astype(f32)
        wide = jnp.concatenate([value, jnp.zeros((8, value.shape[1]), f32)], axis=0)
        for i in range(NX * NS):
            fin_out[i, :, PIECES[piece][0]:PIECES[piece][1]] = wide[i * per:i * per + FINAL].astype(bf16)

    fin_copies = {}
    fin_lanes = ((0, 512), (512, 640))

    def fin_send(part):
        low, high = fin_lanes[part]
        for kx in (2, 1, 3, 0):
            for ks in (2, 1, 3, 0):
                if kx or ks:
                    index = NS * kx + ks
                    to = lax.rem(x + kx, NX) * NS + lax.rem(s + ks, NS)
                    device = {"dp": z * NX + lax.rem(x + kx, NX), "seq": lax.rem(s + ks, NS)}
                    fin_copies[part, index] = send(
                        fin_out.at[to, :, pl.ds(low, high - low)],
                        fin_in.at[index, :, pl.ds(low, high - low)],
                        fin_s.at[part * NX * NS + index], fin_r.at[part * NX * NS + index], device,
                    )

    def fin_sum(part):
        low, high = fin_lanes[part]
        for ks in (1, 3, 2, 0):
            total = None
            for kx in range(NX):
                if kx or ks:
                    fin_copies[part, NS * kx + ks].wait_recv()
                    term = fin_in[NS * kx + ks, :, low:high].astype(f32)
                else:
                    term = fin_out[x * NS + s, :, low:high].astype(f32)
                total = term if total is None else total + term
            grads[lax.rem(s + NS - ks, NS), :, low:high] = total

    head(0)
    pn1[...] = pt_n[:256].T
    pg1[...] = pt_g[:PAD].T
    rs_first(0)
    head(1)
    pg2[...] = pt_g[PAD:].T
    pn2[...] = pt_n[3 * PAD:4 * PAD].T
    rs_first(1)
    pn3[...] = pt_n[4 * PAD:].T
    rs_first(2)
    at_copies = [
        send(
            att.at[rows_of(lax.rem(s + k, NS))], att_all.at[s],
            at_s.at[k - 1], at_r.at[k - 1], at_s_(s + k),
        )
        for k in range(1, NS)
    ]
    att_all[s] = att[mine]
    for piece in range(n):
        rs_step(piece, 1)
    for copy in at_copies:
        copy.wait_recv()
    partial_out = nn(att_all[0], wo_pad[:ATT])
    for i in range(1, NS):
        partial_out += nn(att_all[i], wo_pad[i * ATT:(i + 1) * ATT])
    lo_out[...] = partial_out.astype(bf16)
    lo_copy = send(lo_out, lo_in, lo_s, lo_r, other)
    for piece in range(n):
        rs_step(piece, 2)
    lo_copy.wait_recv()
    both = lo_out[...].astype(f32) + lo_in[...].astype(f32)
    layer_out[:, :HALF] = (pk[0].astype(f32) + both[:, :HALF]).astype(bf16)
    layer_out[:, HALF:] = (pk[1].astype(f32) + both[:, HALF:]).astype(bf16)
    for piece in range(n):
        rs_step(piece, 3)
    rs_last(0)
    rs_last(1)
    fin_send(0)
    rs_last(2)
    fin_send(1)
    fin_sum(0)
    fin_sum(1)
    for copy in started:
        copy.wait_send()


def finish(layer_in, grads, layer_out, qkv, wout):
    per, first, last = OWN // NS, 3 * HEAD, 5 * HEAD
    layer_out[...] = layer_in[...]
    blocks = [grads[i][:per] for i in range(NS)]
    spans = ((0, first), (last, COLS))
    qkv[...] = jnp.concatenate([b[:, low:high] for b in blocks for low, high in spans], axis=1)
    wout[...] = jnp.concatenate([b[:, first:last] for b in blocks], axis=1)


def scratch_shapes(nz):
    far = nz // 2

    def vm(*shape, kind=bf16):
        return pltpu.VMEM(shape, kind)

    def dma(*shape):
        return pltpu.SemaphoreType.DMA(shape)

    one = pltpu.SemaphoreType.DMA
    rings = [vm(2, far, CHUNK, high - low) for low, high in PIECES]
    return [
        vm(1, ROWS // NX, kind=jnp.int32), vm(1, GROUP, kind=jnp.int32), vm(D, kind=f32),
        vm(D, kind=f32),
        vm(ROWS, D), vm(ROWS, D), vm(2, GROUP, HALF), vm(2, ROWS, HALF), vm(2, GROUP, HALF),
        vm(NS, 8, ROWS, kind=f32), vm(D, HALF), vm(D, 6 * PAD), vm(NS * ATT, D),
        vm(GROUP, 6 * PAD), vm(D, GROUP), vm(D, GROUP), vm(GROUP, ATT), vm(ATT, GROUP),
        vm(GROUP, PAD, kind=f32), vm(COLS, GROUP), vm(3 * PAD, GROUP), vm(GROUP, 2 * PAD),
        vm(GROUP, PAD), vm(GROUP, 2 * PAD), vm(GROUP, PAD), vm(GROUP, PAD), vm(GROUP, ATT),
        vm(NS, ROWS, ATT), vm(ROWS, D), vm(ROWS, D),
        *rings, *rings, vm(NX * NS, FINAL, COLS), vm(NX * NS, FINAL, COLS),
        pltpu.SemaphoreType.REGULAR, dma(16), dma(nz - 1), dma(nz - 1), dma(3), dma(3), dma(3),
        dma(3), dma(6), dma(3), one, one, dma(3), dma(3), dma(9), dma(9), dma(6), dma(6), dma(3),
        dma(3), one, one,
        dma(2 * len(PIECES) * far), dma(2 * len(PIECES) * far),
        dma(2 * NX * NS), dma(2 * NX * NS),
    ]


def body(patches, arrivals, segment_ids, norm_gain, norm_bias, w_qkv, w_out, grad_out):
    nz = lax.axis_size("dp") // NX
    anywhere = pl.BlockSpec(memory_space=pl.ANY)
    vmem = pl.BlockSpec(memory_space=pltpu.VMEM)
    layer, grads = pl.pallas_call(
        functools.partial(kernel, nz),
        out_shape=(
            jax.ShapeDtypeStruct((ROWS, D), bf16),
            jax.ShapeDtypeStruct((NS, FINAL, COLS), f32),
        ),
        in_specs=[anywhere] * 8,
        out_specs=(vmem, vmem),
        scratch_shapes=scratch_shapes(nz),
        compiler_params=pltpu.CompilerParams(
            collective_id=0, has_side_effects=True, vmem_limit_bytes=56 * 1024 * 1024
        ),
    )(
        patches, arrivals, segment_ids.reshape(1, GROUP), norm_gain, norm_bias, w_qkv, w_out,
        grad_out,
    )
    per = OWN // NS
    return pl.pallas_call(
        finish,
        out_shape=(
            jax.ShapeDtypeStruct((ROWS, D), bf16),
            jax.ShapeDtypeStruct((per, NS * QKV), f32),
            jax.ShapeDtypeStruct((per, NS * HEADS_OWN * HEAD), f32),
        ),
        in_specs=[vmem, vmem],
        out_specs=(vmem, vmem, vmem),
    )(layer, grads)


def solution(mesh):
    return jax.shard_map(
        body,
        mesh=mesh,
        in_specs=(
            P(("dp", "seq"), None),
            P(("dp", "seq"), None),
            P("dp"),
            P(),
            P(),
            P(None, "tensor"),
            P("tensor", None),
            P(("dp", "seq"), None),
        ),
        out_specs=(P(("dp", "seq"), None), P(("dp", "seq"), "tensor"), P(("dp", "seq"), "tensor")),
        check_vma=False,
    )
```

```python
import functools

import jax
import jax.numpy as jnp
from jax import lax
from jax.experimental import pallas as pl
from jax.experimental.pallas import tpu as pltpu
from jax.sharding import PartitionSpec as P

HEAD = 80
PAD = 128
HEADS_OWN = 2
NX = 4
NS = 4
ROWS = 128
D = 1280
HALF = D // 2
GROUP = NS * ROWS
QKV = 3 * HEADS_OWN * HEAD
ATT = HEADS_OWN * PAD
COLS = 4 * HEADS_OWN * HEAD
PIECES = ((0, 256), (256, 640))
CHUNK = 160
OWN = 40
FINAL = 16
epsilon = 1e-06
big_negative = -1e30
MESH = pl.DeviceIdType.MESH
bf16 = jnp.bfloat16
f32 = jnp.float32


def nn(a, b):
    return jnp.dot(a, b, preferred_element_type=f32)


def nt(a, b):
    return lax.dot_general(a, b, (((1,), (1,)), ((), ())), preferred_element_type=f32)


def iota(shape, axis):
    return lax.broadcasted_iota(jnp.int32, shape, axis)


def kernel(nz, patches, arrivals, seg, gain, bias, w_qkv, w_out, gout, layer_out, grads, *scratch):
    (arrivals_v, seg_v, gain_v, bias_v, az, xs_out, raw, pk, gall, tgt, w_win, w_pad, wo_pad, proj, n_t, go_t, ga, ga_t, segk,
     pt_n, pt_g, pn1, pg1, pg2, pn2, pn3, att, att_all, lo_out, lo_in) = scratch[:30]
    n = len(PIECES)
    rs_out, rs_in = scratch[30:30 + n], scratch[30 + n:30 + 2 * n]
    (fin_out, fin_in, loc, az_s, az_r, gy_s, gy_r, gf_s, gf_r, ax_s, ax_r, tg_s, tg_r, ry_s, ry_r,
     rf_s, rf_r, at_s, at_r, lo_s, lo_r, rs_s, rs_r, fin_s, fin_r) = scratch[30 + 2 * n:]
    dp, s, c = lax.axis_index("dp"), lax.axis_index("seq"), lax.axis_index("tensor")
    z, x = lax.div(dp, NX), lax.rem(dp, NX)
    started, gone = [], []

    def at_z(zt):
        return {"dp": lax.rem(zt + nz, nz) * NX + x}

    def at_x(xt):
        return {"dp": z * NX + lax.rem(xt + NX, NX)}

    def at_s_(st):
        return {"seq": lax.rem(st + NS, NS)}

    other = {"tensor": 1 - c}

    barrier = pltpu.get_barrier_semaphore()
    far = nz // 2
    partners = (
        [at_z(z + k) for k in sorted(range(1, nz), key=lambda k: abs(k - far))]
        + [at_x(x + k) for k in (2, 1, 3)]
        + [at_s_(s + k) for k in (2, 1, 3)]
        + [other]
    )
    for device in partners:
        pl.semaphore_signal(barrier, inc=1, device_id=device, device_id_type=MESH)

    def send(src, dst, ssem, rsem, device):
        copy = pltpu.make_async_remote_copy(
            src_ref=src, dst_ref=dst, send_sem=ssem, recv_sem=rsem, device_id=device,
            device_id_type=MESH,
        )
        copy.start()
        started.append(copy)
        return copy

    def fetch(src, dst, sem):
        copy = pltpu.make_async_copy(src, dst, sem)
        copy.start()
        return copy

    cols = pl.ds(pl.multiple_of(c * HALF, HALF), HALF)
    mine = pl.ds(pl.multiple_of(s * ROWS, ROWS), ROWS)

    own_patch = fetch(
        patches.at[pl.ds(pl.multiple_of(z * 16, 16), 16), cols],
        az.at[pl.ds(pl.multiple_of(z * 16, 16), 16)], loc.at[0],
    )
    small = [
        fetch(a, b, loc.at[12 + i])
        for i, (a, b) in enumerate(
            ((arrivals, arrivals_v), (seg, seg_v), (gain, gain_v), (bias, bias_v))
        )
    ]
    w_start = lax.min(lax.div(QKV * s, 128) * 128, 3 * D // 2 - HALF)
    w_off = QKV * s - w_start
    w_copy = fetch(w_qkv.at[:, pl.ds(pl.multiple_of(w_start, 128), HALF)], w_win, loc.at[3])
    own_gout = [
        fetch(gout.at[:, pl.ds(i * HALF, HALF)], gall.at[i, mine], loc.at[1 + i]) for i in range(2)
    ]
    wo_copies = [
        fetch(w_out.at[pl.ds(i * HEAD, HEAD)], wo_pad.at[pl.ds(i * PAD, HEAD)], loc.at[4 + i])
        for i in range(NS * HEADS_OWN)
    ]
    pl.semaphore_wait(barrier, len(partners))

    az_copies = []
    for k in sorted(range(1, nz), key=lambda k: abs(k - far)):
        zt = lax.rem(z + k, nz)
        az_copies.append(send(
            patches.at[pl.ds(pl.multiple_of(zt * 16, 16), 16), cols],
            az.at[pl.ds(pl.multiple_of(z * 16, 16), 16)],
            az_s.at[k - 1], az_r.at[k - 1], at_z(z + k),
        ))
    gy_copies = {
        k: send(gout.at[:, cols], gall.at[c, mine], gy_s.at[k - 1], gy_r.at[k - 1], at_s_(s + k))
        for k in (1, 3, 2)
    }

    for copy in small:
        copy.wait()

    row, col = iota((ROWS, ROWS), 0), iota((ROWS, ROWS), 1)
    to_x = (x + (row >> 5)) & (NX - 1)
    perm = (col == ((row >> 2) & 7) * 16 + to_x * 4 + (row & 3)).astype(bf16)
    slot = iota((32, ROWS), 1)
    origin = ((slot >> 2) & 7) * NX + ((x + (slot >> 5)) & (NX - 1))
    counter = iota((32, ROWS), 0)
    counts = jnp.broadcast_to(arrivals_v[...].astype(f32), (16, 32)).astype(bf16)
    starts = nn(counts, (counter < origin).astype(bf16))[0:8]
    number = nn(counts, (counter == origin).astype(bf16))[0:8]
    place = (iota((8, ROWS), 1) & 3).astype(f32)
    tgt[s] = jnp.where(place < number, starts + place, -1.0)
    tg_copies = {
        k: send(tgt.at[s], tgt.at[s], tg_s.at[k - 1], tg_r.at[k - 1], at_s_(s + k))
        for k in (1, 3, 2)
    }

    ids = seg_v[...].astype(f32)
    key_ids = jnp.where(ids < 0.0, -2.0, ids)
    segk[...] = jnp.broadcast_to(key_ids, (PAD, GROUP)).T

    for i in range(NS * HEADS_OWN):
        wo_pad[i * PAD + HEAD:(i + 1) * PAD] = jnp.zeros((PAD - HEAD, D), bf16)
    pt_n[3 * HEAD:5 * HEAD] = jnp.zeros((2 * HEAD, GROUP), bf16)
    pt_g[...] = jnp.zeros(pt_g.shape, bf16)

    w_copy.wait()

    def pad_pair(i, carry):
        r, cc = iota((HALF, 2 * PAD), 0), iota((HALF, 2 * PAD), 1)
        d = cc & (PAD - 1)
        wanted = w_off + (2 * i + (cc >> 7)) * HEAD + d
        chosen = ((r == wanted) & (d < HEAD)).astype(bf16)
        out = pl.ds(pl.multiple_of(i * 2 * PAD, 2 * PAD), 2 * PAD)
        w_pad[:, out] = nn(w_win[...], chosen).astype(bf16)
        return carry

    lax.fori_loop(0, 3, pad_pair, 0)

    own_patch.wait()
    for copy in az_copies:
        copy.wait_recv()
    xs = nn(perm, az[...]).astype(bf16)
    quarter = ROWS // NX
    xs_out[...] = xs
    raw[c, pl.ds(pl.multiple_of(s * ROWS, ROWS), quarter)] = xs[:quarter]
    ax_copies = []
    for k in (1, 3, 2):
        landing = pl.multiple_of(s * ROWS + (NX - k) * quarter, quarter)
        ax_copies.append(send(
            xs_out.at[pl.ds(k * quarter, quarter)], raw.at[c, pl.ds(landing, quarter)],
            ax_s.at[k - 1], ax_r.at[k - 1], at_x(x + k),
        ))
    first = pl.ds(pl.multiple_of(s * ROWS, ROWS), quarter)
    rest = pl.ds(pl.multiple_of(s * ROWS + quarter, quarter), ROWS - quarter)
    ry_copies, rf_copies = {}, {}

    def spread(part, block):
        for k in (1, 3, 2):
            ry_copies[part, k] = send(
                raw.at[c, block], raw.at[c, block], ry_s.at[3 * part + k - 1],
                ry_r.at[3 * part + k - 1], at_s_(s + k),
            )
        rf_copies[part] = send(
            raw.at[c, block], raw.at[c, block], rf_s.at[part], rf_r.at[part], other
        )

    spread(0, first)
    for copy in ax_copies:
        copy.wait_recv()
    spread(1, rest)

    def peer(k):
        return lax.rem(s + NS - k, NS)

    def rows_of(index):
        return pl.ds(pl.multiple_of(index * ROWS, ROWS), ROWS)

    def take(index):
        block = rows_of(index)
        pick = (row.astype(f32) == tgt[index][0:1]).astype(bf16)
        x0, x1 = nn(pick, raw[0, block]), nn(pick, raw[1, block])
        y0, y1 = x0, x1
        mean = (jnp.sum(x0, axis=1, keepdims=True) + jnp.sum(x1, axis=1, keepdims=True)) / D
        x0, x1 = x0 - mean, x1 - mean
        var = (jnp.sum(x0 * x0, axis=1, keepdims=True) + jnp.sum(x1 * x1, axis=1, keepdims=True)) / D
        inv = lax.rsqrt(var + epsilon)
        gains, biases = gain_v[...].reshape(1, D), bias_v[...].reshape(1, D)
        x0 = (x0 * inv * gains[:, :HALF] + biases[:, :HALF]).astype(bf16)
        x1 = (x1 * inv * gains[:, HALF:] + biases[:, HALF:]).astype(bf16)
        proj[block] = (nn(x0, w_pad[:HALF]) + nn(x1, w_pad[HALF:])).astype(bf16)
        n_t[:HALF, block] = x0.T
        n_t[HALF:, block] = x1.T
        return y0, y1

    gf_copies = []
    for k in (1, 3, 2):
        gy_copies[k].wait_recv()
        block = rows_of(peer(k))
        gf_copies.append(send(
            gall.at[c, block], gall.at[c, block], gf_s.at[k - 1], gf_r.at[k - 1], other
        ))
    for part in range(2):
        rf_copies[part].wait_recv()
    own0, own1 = take(s)
    pk[0] = own0.astype(bf16)
    pk[1] = own1.astype(bf16)
    for copy in wo_copies:
        copy.wait()
    for copy in own_gout:
        copy.wait()
    for copy in gf_copies:
        copy.wait_recv()
    wo_mine = wo_pad[pl.ds(pl.multiple_of(s * ATT, ATT), ATT)]
    ga[...] = (nt(gall[0], wo_mine[:, :HALF]) + nt(gall[1], wo_mine[:, HALF:])).astype(bf16)
    ga_t[...] = (nt(wo_mine[:, :HALF], gall[0]) + nt(wo_mine[:, HALF:], gall[1])).astype(bf16)
    go_t[:HALF] = gall[0].T
    go_t[HALF:] = gall[1].T

    def pass_on(k):
        for part in range(2):
            ry_copies[part, k].wait_recv()
        tg_copies[k].wait_recv()
        block = rows_of(peer(k))
        rf_copies[1 + k] = send(
            raw.at[c, block], raw.at[c, block], rf_s.at[1 + k], rf_r.at[1 + k], other
        )

    def take_peer(k):
        rf_copies[1 + k].wait_recv()
        take(peer(k))

    pass_on(1)
    pass_on(3)
    take_peer(1)
    take_peer(3)
    pass_on(2)
    take_peer(2)

    scale = HEAD ** (-0.5)
    to_exp2 = scale * 1.4426950408889634
    query_ids = ids

    def head(h):
        base = 3 * PAD * h
        k_, v_ = proj[:, base + PAD:base + 2 * PAD], proj[:, base + 2 * PAD:base + 3 * PAD]
        k_t, v_t = k_.T, v_.T
        wide = 256
        parts = [slice(b * wide, (b + 1) * wide) for b in range(GROUP // wide)]
        keys = jnp.concatenate([segk[...]] * (wide // PAD), axis=1)
        q_ = [proj[part, base:base + PAD] for part in parts]
        g_ = [ga[part, h * PAD:(h + 1) * PAD] for part in parts]
        scores = [nt(k_, q) for q in q_]
        d_weights = [nt(v_, g) for g in g_]
        raised, share = [], []
        for part, score in zip(parts, scores):
            masked = jnp.where(keys == query_ids[:, part], score, big_negative)
            top = jnp.max(masked, axis=0, keepdims=True)
            up = jnp.exp2((masked - top) * to_exp2)
            total = jnp.sum(up, axis=0, keepdims=True)
            raised.append(up)
            share.append(jnp.where(query_ids[:, part] < 0.0, 0.0, 1.0 / total))
        d_k = d_v = None
        start = 0 if h == 0 else 5 * HEAD
        out_at = 3 * HEAD - PAD + h * HEAD
        for part, q, g, up, sh, dw in zip(parts, q_, g_, raised, share, d_weights):
            g_t = ga_t[h * PAD:(h + 1) * PAD, part]
            exact = up * sh
            weights = exact.astype(bf16)
            out_t = nn(v_t, weights).astype(bf16)
            term = nn(weights, g)
            d_v = term if d_v is None else d_v + term
            delta = jnp.sum(g_t.astype(f32) * out_t.astype(f32), axis=0, keepdims=True)
            d_scores = (exact * (dw - delta) * scale).astype(bf16)
            dq_t = nn(k_t, d_scores).astype(bf16)
            term = nn(d_scores, q)
            d_k = term if d_k is None else d_k + term
            pt_n[start:start + HEAD, part] = dq_t[:HEAD]
            pt_g[out_at:out_at + HEAD, part] = out_t[:HEAD]
            att[part, h * PAD:(h + 1) * PAD] = out_t.T
        pt_n[start + HEAD:start + 2 * HEAD] = d_k.T[:HEAD].astype(bf16)
        pt_n[start + 2 * HEAD:start + 3 * HEAD] = d_v.T[:HEAD].astype(bf16)

    def chunk(piece, zc):
        block = pl.ds(pl.multiple_of(lax.rem(zc + 2 * nz, nz) * CHUNK, 16), CHUNK)
        if piece == 0:
            a = nn(n_t[block], pn1[...])
            b = nn(go_t[block], pg1[...])
            return jnp.concatenate([a[:, :PAD], a[:, PAD:] + b], axis=1)
        if piece == 1:
            b = nn(go_t[block], pg2[...])
            a = nn(n_t[block], pn2[...])
            last = nn(n_t[block], pn3[...])
            return jnp.concatenate([b[:, :PAD], b[:, PAD:] + a, last], axis=1)

    rs_copies = {}
    mid = CHUNK // 2

    def rs_send(piece, way, step, part):
        index = (piece * 2 + way) * far + step
        rs_copies[piece, way, step] = send(
            rs_out[piece].at[way, step, part], rs_in[piece].at[way, step, part],
            rs_s.at[index], rs_r.at[index], at_z(z + 1) if way == 0 else at_z(z + nz - 1),
        )

    def rs_first(piece):
        value = chunk(piece, z + far).astype(bf16)
        rs_out[piece][0, 0, :mid] = value[:mid]
        rs_out[piece][1, 0, mid:] = value[mid:]
        rs_send(piece, 0, 0, pl.ds(0, mid))
        rs_send(piece, 1, 0, pl.ds(mid, mid))

    def rs_step(piece, step):
        for way in range(2):
            value = chunk(piece, z + far - step if way == 0 else z - far + step)
            rs_copies[piece, way, step - 1].wait_recv()
            if step == 1:
                if way == 0:
                    got = rs_in[piece][0, 0, :mid].astype(f32)
                    value = jnp.concatenate([value[:mid] + got, value[mid:]], axis=0)
                else:
                    got = rs_in[piece][1, 0, mid:].astype(f32)
                    value = jnp.concatenate([value[:mid], value[mid:] + got], axis=0)
            else:
                value = value + rs_in[piece][way, step - 1].astype(f32)
            rs_out[piece][way, step] = value.astype(bf16)
            rs_send(piece, way, step, pl.ds(0, CHUNK))

    per = OWN // NS

    def rs_last(piece):
        value = chunk(piece, z)
        for way in range(2):
            rs_copies[piece, way, far - 1].wait_recv()
            value = value + rs_in[piece][way, far - 1].astype(f32)
        wide = jnp.concatenate([value, jnp.zeros((8, value.shape[1]), f32)], axis=0)
        for i in range(NX * NS):
            fin_out[i, :, PIECES[piece][0]:PIECES[piece][1]] = wide[i * per:i * per + FINAL].astype(bf16)

    fin_copies = {}
    fin_lanes = PIECES

    def fin_send(part):
        low, high = fin_lanes[part]
        for kx in (2, 1, 3, 0):
            for ks in (2, 1, 3, 0):
                if kx or ks:
                    index = NS * kx + ks
                    to = lax.rem(x + kx, NX) * NS + lax.rem(s + ks, NS)
                    device = {"dp": z * NX + lax.rem(x + kx, NX), "seq": lax.rem(s + ks, NS)}
                    fin_copies[part, index] = send(
                        fin_out.at[to, :, pl.ds(low, high - low)],
                        fin_in.at[index, :, pl.ds(low, high - low)],
                        fin_s.at[part * NX * NS + index], fin_r.at[part * NX * NS + index], device,
                    )

    def fin_sum(part):
        low, high = fin_lanes[part]
        for ks in (1, 3, 2, 0):
            total = None
            for kx in range(NX):
                if kx or ks:
                    fin_copies[part, NS * kx + ks].wait_recv()
                    term = fin_in[NS * kx + ks, :, low:high].astype(f32)
                else:
                    term = fin_out[x * NS + s, :, low:high].astype(f32)
                total = term if total is None else total + term
            grads[lax.rem(s + NS - ks, NS), :, low:high] = total

    head(0)
    pn1[...] = pt_n[:256].T
    pg1[...] = pt_g[:PAD].T
    rs_first(0)
    head(1)
    pg2[...] = pt_g[PAD:].T
    pn2[...] = pt_n[3 * PAD:4 * PAD].T
    pn3[...] = pt_n[4 * PAD:].T
    rs_first(1)
    at_copies = [
        send(
            att.at[rows_of(lax.rem(s + k, NS))], att_all.at[s],
            at_s.at[k - 1], at_r.at[k - 1], at_s_(s + k),
        )
        for k in range(1, NS)
    ]
    att_all[s] = att[mine]
    for piece in range(n):
        rs_step(piece, 1)
    for copy in at_copies:
        copy.wait_recv()
    partial_out = nn(att_all[0], wo_pad[:ATT])
    for i in range(1, NS):
        partial_out += nn(att_all[i], wo_pad[i * ATT:(i + 1) * ATT])
    lo_out[...] = partial_out.astype(bf16)
    lo_copy = send(lo_out, lo_in, lo_s, lo_r, other)
    for piece in range(n):
        rs_step(piece, 2)
    lo_copy.wait_recv()
    both = lo_out[...].astype(f32) + lo_in[...].astype(f32)
    layer_out[:, :HALF] = (pk[0].astype(f32) + both[:, :HALF]).astype(bf16)
    layer_out[:, HALF:] = (pk[1].astype(f32) + both[:, HALF:]).astype(bf16)
    for piece in range(n):
        rs_step(piece, 3)
    rs_last(0)
    fin_send(0)
    rs_last(1)
    fin_send(1)
    fin_sum(0)
    fin_sum(1)
    for copy in started:
        if not any(copy is other_copy for other_copy in gone):
            copy.wait_send()


def finish(layer_in, grads, layer_out, qkv, wout):
    per, first, last = OWN // NS, 3 * HEAD, 5 * HEAD
    layer_out[...] = layer_in[...]
    blocks = [grads[i][:per] for i in range(NS)]
    spans = ((0, first), (last, COLS))
    qkv[...] = jnp.concatenate([b[:, low:high] for b in blocks for low, high in spans], axis=1)
    wout[...] = jnp.concatenate([b[:, first:last] for b in blocks], axis=1)


def scratch_shapes(nz):
    far = nz // 2

    def vm(*shape, kind=bf16):
        return pltpu.VMEM(shape, kind)

    def dma(*shape):
        return pltpu.SemaphoreType.DMA(shape)

    one = pltpu.SemaphoreType.DMA
    rings = [vm(2, far, CHUNK, high - low) for low, high in PIECES]
    return [
        vm(1, ROWS // NX, kind=jnp.int32), vm(1, GROUP, kind=jnp.int32), vm(D, kind=f32),
        vm(D, kind=f32),
        vm(ROWS, HALF), vm(ROWS, HALF), vm(2, GROUP, HALF), vm(2, ROWS, HALF), vm(2, GROUP, HALF),
        vm(NS, 8, ROWS, kind=f32), vm(D, HALF), vm(D, 6 * PAD), vm(NS * ATT, D),
        vm(GROUP, 6 * PAD), vm(D, GROUP), vm(D, GROUP), vm(GROUP, ATT), vm(ATT, GROUP),
        vm(GROUP, PAD, kind=f32), vm(COLS, GROUP), vm(3 * PAD, GROUP), vm(GROUP, 2 * PAD),
        vm(GROUP, PAD), vm(GROUP, 2 * PAD), vm(GROUP, PAD), vm(GROUP, PAD), vm(GROUP, ATT),
        vm(NS, ROWS, ATT), vm(ROWS, D), vm(ROWS, D),
        *rings, *rings, vm(NX * NS, FINAL, COLS), vm(NX * NS, FINAL, COLS),
        dma(16), dma(nz - 1), dma(nz - 1), dma(3), dma(3), dma(3), dma(3), dma(3), dma(3),
        dma(3), dma(3), dma(6), dma(6), dma(5), dma(5), dma(3), dma(3), one, one,
        dma(2 * len(PIECES) * far), dma(2 * len(PIECES) * far),
        dma(2 * NX * NS), dma(2 * NX * NS),
    ]


def body(patches, arrivals, segment_ids, norm_gain, norm_bias, w_qkv, w_out, grad_out):
    nz = lax.axis_size("dp") // NX
    anywhere = pl.BlockSpec(memory_space=pl.ANY)
    vmem = pl.BlockSpec(memory_space=pltpu.VMEM)
    layer, grads = pl.pallas_call(
        functools.partial(kernel, nz),
        out_shape=(
            jax.ShapeDtypeStruct((ROWS, D), bf16),
            jax.ShapeDtypeStruct((NS, FINAL, COLS), f32),
        ),
        in_specs=[anywhere] * 8,
        out_specs=(vmem, vmem),
        scratch_shapes=scratch_shapes(nz),
        compiler_params=pltpu.CompilerParams(
            collective_id=0, has_side_effects=True, vmem_limit_bytes=56 * 1024 * 1024
        ),
    )(
        patches, arrivals, segment_ids.reshape(1, GROUP), norm_gain, norm_bias, w_qkv, w_out,
        grad_out,
    )
    per = OWN // NS
    return pl.pallas_call(
        finish,
        out_shape=(
            jax.ShapeDtypeStruct((ROWS, D), bf16),
            jax.ShapeDtypeStruct((per, NS * QKV), f32),
            jax.ShapeDtypeStruct((per, NS * HEADS_OWN * HEAD), f32),
        ),
        in_specs=[vmem, vmem],
        out_specs=(vmem, vmem, vmem),
    )(layer, grads)


def solution(mesh):
    return jax.shard_map(
        body,
        mesh=mesh,
        in_specs=(
            P(("dp", "seq"), None),
            P(("dp", "seq"), None),
            P("dp"),
            P(),
            P(),
            P(None, "tensor"),
            P("tensor", None),
            P(("dp", "seq"), None),
        ),
        out_specs=(P(("dp", "seq"), None), P(("dp", "seq"), "tensor"), P(("dp", "seq"), "tensor")),
        check_vma=False,
    )
```

```python
import functools

import jax
import jax.numpy as jnp
from jax import lax
from jax.experimental import pallas as pl
from jax.experimental.pallas import tpu as pltpu
from jax.sharding import PartitionSpec as P

HEAD = 80
PAD = 128
HEADS_OWN = 2
NX = 4
NS = 4
ROWS = 128
D = 1280
HALF = D // 2
GROUP = NS * ROWS
QKV = 3 * HEADS_OWN * HEAD
ATT = HEADS_OWN * PAD
COLS = 4 * HEADS_OWN * HEAD
PIECES = ((0, 256), (256, 640))
CHUNK = 160
OWN = 40
FINAL = 16
epsilon = 1e-06
big_negative = -1e30
MESH = pl.DeviceIdType.MESH
bf16 = jnp.bfloat16
f32 = jnp.float32


def nn(a, b):
    return jnp.dot(a, b, preferred_element_type=f32)


def nt(a, b):
    return lax.dot_general(a, b, (((1,), (1,)), ((), ())), preferred_element_type=f32)


def iota(shape, axis):
    return lax.broadcasted_iota(jnp.int32, shape, axis)


def kernel(nz, patches, arrivals, seg, gain, bias, w_qkv, w_out, gout, layer_out, grads, *scratch):
    (arrivals_v, seg_v, gain_v, bias_v, az, xs_out, raw, pk, gall, tgt, w_win, w_pad, wo_pad, proj, n_t, go_t, ga, ga_t, segk,
     pt_n, pt_g, pn1, pg1, pg2, pn2, pn3, att, att_all, lo_out, lo_in) = scratch[:30]
    n = len(PIECES)
    rs_out, rs_in = scratch[30:30 + n], scratch[30 + n:30 + 2 * n]
    (fin_out, fin_in, loc, az_s, az_r, gy_s, gy_r, gf_s, gf_r, ax_s, ax_r, tg_s, tg_r, ry_s, ry_r,
     rf_s, rf_r, at_s, at_r, lo_s, lo_r, rs_s, rs_r, fin_s, fin_r) = scratch[30 + 2 * n:]
    dp, s, c = lax.axis_index("dp"), lax.axis_index("seq"), lax.axis_index("tensor")
    z, x = lax.div(dp, NX), lax.rem(dp, NX)
    started, gone = [], []

    def at_z(zt):
        return {"dp": lax.rem(zt + nz, nz) * NX + x}

    def at_x(xt):
        return {"dp": z * NX + lax.rem(xt + NX, NX)}

    def at_s_(st):
        return {"seq": lax.rem(st + NS, NS)}

    other = {"tensor": 1 - c}

    barrier = pltpu.get_barrier_semaphore()
    far = nz // 2
    partners = (
        [at_z(z + k) for k in sorted(range(1, nz), key=lambda k: abs(k - far))]
        + [at_x(x + k) for k in (2, 1, 3)]
        + [at_s_(s + k) for k in (2, 1, 3)]
        + [other]
    )
    for device in partners:
        pl.semaphore_signal(barrier, inc=1, device_id=device, device_id_type=MESH)

    def send(src, dst, ssem, rsem, device):
        copy = pltpu.make_async_remote_copy(
            src_ref=src, dst_ref=dst, send_sem=ssem, recv_sem=rsem, device_id=device,
            device_id_type=MESH,
        )
        copy.start()
        started.append(copy)
        return copy

    def fetch(src, dst, sem):
        copy = pltpu.make_async_copy(src, dst, sem)
        copy.start()
        return copy

    cols = pl.ds(pl.multiple_of(c * HALF, HALF), HALF)
    mine = pl.ds(pl.multiple_of(s * ROWS, ROWS), ROWS)

    own_patch = fetch(
        patches.at[pl.ds(pl.multiple_of(z * 16, 16), 16), cols],
        az.at[pl.ds(pl.multiple_of(z * 16, 16), 16)], loc.at[0],
    )
    small = [
        fetch(a, b, loc.at[12 + i])
        for i, (a, b) in enumerate(
            ((arrivals, arrivals_v), (seg, seg_v), (gain, gain_v), (bias, bias_v))
        )
    ]
    w_start = lax.min(lax.div(QKV * s, 128) * 128, 3 * D // 2 - HALF)
    w_off = QKV * s - w_start
    w_copy = fetch(w_qkv.at[:, pl.ds(pl.multiple_of(w_start, 128), HALF)], w_win, loc.at[3])
    own_gout = [
        fetch(gout.at[:, pl.ds(i * HALF, HALF)], gall.at[i, mine], loc.at[1 + i]) for i in range(2)
    ]
    wo_copies = [
        fetch(w_out.at[pl.ds(i * HEAD, HEAD)], wo_pad.at[pl.ds(i * PAD, HEAD)], loc.at[4 + i])
        for i in range(NS * HEADS_OWN)
    ]
    pl.semaphore_wait(barrier, len(partners))

    az_copies = []
    for k in sorted(range(1, nz), key=lambda k: abs(k - far)):
        zt = lax.rem(z + k, nz)
        az_copies.append(send(
            patches.at[pl.ds(pl.multiple_of(zt * 16, 16), 16), cols],
            az.at[pl.ds(pl.multiple_of(z * 16, 16), 16)],
            az_s.at[k - 1], az_r.at[k - 1], at_z(z + k),
        ))
    gy_copies = {
        k: send(gout.at[:, cols], gall.at[c, mine], gy_s.at[k - 1], gy_r.at[k - 1], at_s_(s + k))
        for k in (1, 3, 2)
    }

    for copy in small:
        copy.wait()

    row, col = iota((ROWS, ROWS), 0), iota((ROWS, ROWS), 1)
    to_x = (x + (row >> 5)) & (NX - 1)
    perm = (col == ((row >> 2) & 7) * 16 + to_x * 4 + (row & 3)).astype(bf16)
    slot = iota((32, ROWS), 1)
    origin = ((slot >> 2) & 7) * NX + ((x + (slot >> 5)) & (NX - 1))
    counter = iota((32, ROWS), 0)
    counts = jnp.broadcast_to(arrivals_v[...].astype(f32), (16, 32)).astype(bf16)
    starts = nn(counts, (counter < origin).astype(bf16))[0:8]
    number = nn(counts, (counter == origin).astype(bf16))[0:8]
    place = (iota((8, ROWS), 1) & 3).astype(f32)
    tgt[s] = jnp.where(place < number, starts + place, -1.0)
    tg_copies = {
        k: send(tgt.at[s], tgt.at[s], tg_s.at[k - 1], tg_r.at[k - 1], at_s_(s + k))
        for k in (1, 3, 2)
    }

    ids = seg_v[...].astype(f32)
    key_ids = jnp.where(ids < 0.0, -2.0, ids)
    segk[...] = jnp.broadcast_to(key_ids, (PAD, GROUP)).T

    for i in range(NS * HEADS_OWN):
        wo_pad[i * PAD + HEAD:(i + 1) * PAD] = jnp.zeros((PAD - HEAD, D), bf16)
    pt_n[3 * HEAD:5 * HEAD] = jnp.zeros((2 * HEAD, GROUP), bf16)
    pt_g[...] = jnp.zeros(pt_g.shape, bf16)

    w_copy.wait()

    def pad_pair(i, carry):
        r, cc = iota((HALF, 2 * PAD), 0), iota((HALF, 2 * PAD), 1)
        d = cc & (PAD - 1)
        wanted = w_off + (2 * i + (cc >> 7)) * HEAD + d
        chosen = ((r == wanted) & (d < HEAD)).astype(bf16)
        out = pl.ds(pl.multiple_of(i * 2 * PAD, 2 * PAD), 2 * PAD)
        w_pad[:, out] = nn(w_win[...], chosen).astype(bf16)
        return carry

    lax.fori_loop(0, 3, pad_pair, 0)

    own_patch.wait()
    for copy in az_copies:
        copy.wait_recv()
    xs = nn(perm, az[...]).astype(bf16)
    quarter = ROWS // NX
    xs_out[...] = xs
    raw[c, pl.ds(pl.multiple_of(s * ROWS, ROWS), quarter)] = xs[:quarter]
    ax_copies = []
    for k in (1, 3, 2):
        landing = pl.multiple_of(s * ROWS + (NX - k) * quarter, quarter)
        ax_copies.append(send(
            xs_out.at[pl.ds(k * quarter, quarter)], raw.at[c, pl.ds(landing, quarter)],
            ax_s.at[k - 1], ax_r.at[k - 1], at_x(x + k),
        ))
    first = pl.ds(pl.multiple_of(s * ROWS, ROWS), quarter)
    rest = pl.ds(pl.multiple_of(s * ROWS + quarter, quarter), ROWS - quarter)
    ry_copies, rf_copies = {}, {}

    def spread(part, block):
        for k in (1, 3, 2):
            ry_copies[part, k] = send(
                raw.at[c, block], raw.at[c, block], ry_s.at[3 * part + k - 1],
                ry_r.at[3 * part + k - 1], at_s_(s + k),
            )
        rf_copies[part] = send(
            raw.at[c, block], raw.at[c, block], rf_s.at[part], rf_r.at[part], other
        )

    spread(0, first)
    for copy in ax_copies:
        copy.wait_recv()
    spread(1, rest)

    def peer(k):
        return lax.rem(s + NS - k, NS)

    def rows_of(index):
        return pl.ds(pl.multiple_of(index * ROWS, ROWS), ROWS)

    def take(index):
        block = rows_of(index)
        pick = (row.astype(f32) == tgt[index][0:1]).astype(bf16)
        x0, x1 = nn(pick, raw[0, block]), nn(pick, raw[1, block])
        y0, y1 = x0, x1
        mean = (jnp.sum(x0, axis=1, keepdims=True) + jnp.sum(x1, axis=1, keepdims=True)) / D
        x0, x1 = x0 - mean, x1 - mean
        var = (jnp.sum(x0 * x0, axis=1, keepdims=True) + jnp.sum(x1 * x1, axis=1, keepdims=True)) / D
        inv = lax.rsqrt(var + epsilon)
        gains, biases = gain_v[...].reshape(1, D), bias_v[...].reshape(1, D)
        x0 = (x0 * inv * gains[:, :HALF] + biases[:, :HALF]).astype(bf16)
        x1 = (x1 * inv * gains[:, HALF:] + biases[:, HALF:]).astype(bf16)
        proj[block] = (nn(x0, w_pad[:HALF]) + nn(x1, w_pad[HALF:])).astype(bf16)
        n_t[:HALF, block] = x0.T
        n_t[HALF:, block] = x1.T
        return y0, y1

    gf_copies = []
    for k in (1, 3, 2):
        gy_copies[k].wait_recv()
        block = rows_of(peer(k))
        gf_copies.append(send(
            gall.at[c, block], gall.at[c, block], gf_s.at[k - 1], gf_r.at[k - 1], other
        ))
    for part in range(2):
        rf_copies[part].wait_recv()
    own0, own1 = take(s)
    pk[0] = own0.astype(bf16)
    pk[1] = own1.astype(bf16)
    for copy in wo_copies:
        copy.wait()
    for copy in own_gout:
        copy.wait()
    for copy in gf_copies:
        copy.wait_recv()
    wo_mine = wo_pad[pl.ds(pl.multiple_of(s * ATT, ATT), ATT)]
    ga[...] = (nt(gall[0], wo_mine[:, :HALF]) + nt(gall[1], wo_mine[:, HALF:])).astype(bf16)
    ga_t[...] = (nt(wo_mine[:, :HALF], gall[0]) + nt(wo_mine[:, HALF:], gall[1])).astype(bf16)

    def pass_on(k):
        for part in range(2):
            ry_copies[part, k].wait_recv()
        tg_copies[k].wait_recv()
        block = rows_of(peer(k))
        rf_copies[1 + k] = send(
            raw.at[c, block], raw.at[c, block], rf_s.at[1 + k], rf_r.at[1 + k], other
        )

    def take_peer(k):
        rf_copies[1 + k].wait_recv()
        take(peer(k))

    pass_on(1)
    pass_on(3)
    pass_on(2)
    take_peer(1)
    take_peer(3)
    go_t[:HALF] = gall[0].T
    go_t[HALF:] = gall[1].T
    take_peer(2)

    scale = HEAD ** (-0.5)
    to_exp2 = scale * 1.4426950408889634
    query_ids = ids

    def head(h):
        base = 3 * PAD * h
        k_, v_ = proj[:, base + PAD:base + 2 * PAD], proj[:, base + 2 * PAD:base + 3 * PAD]
        k_t, v_t = k_.T, v_.T
        wide = 256
        parts = [slice(b * wide, (b + 1) * wide) for b in range(GROUP // wide)]
        keys = jnp.concatenate([segk[...]] * (wide // PAD), axis=1)
        q_ = [proj[part, base:base + PAD] for part in parts]
        g_ = [ga[part, h * PAD:(h + 1) * PAD] for part in parts]
        scores = [nt(k_, q) for q in q_]
        d_weights = [nt(v_, g) for g in g_]
        raised, share = [], []
        for part, score in zip(parts, scores):
            masked = jnp.where(keys == query_ids[:, part], score, big_negative)
            top = jnp.max(masked, axis=0, keepdims=True)
            up = jnp.exp2((masked - top) * to_exp2)
            total = jnp.sum(up, axis=0, keepdims=True)
            raised.append(up)
            share.append(jnp.where(query_ids[:, part] < 0.0, 0.0, 1.0 / total))
        d_k = d_v = None
        start = 0 if h == 0 else 5 * HEAD
        out_at = 3 * HEAD - PAD + h * HEAD
        for part, q, g, up, sh, dw in zip(parts, q_, g_, raised, share, d_weights):
            g_t = ga_t[h * PAD:(h + 1) * PAD, part]
            exact = up * sh
            weights = exact.astype(bf16)
            out_t = nn(v_t, weights).astype(bf16)
            term = nn(weights, g)
            d_v = term if d_v is None else d_v + term
            delta = jnp.sum(g_t.astype(f32) * out_t.astype(f32), axis=0, keepdims=True)
            d_scores = (exact * (dw - delta) * scale).astype(bf16)
            dq_t = nn(k_t, d_scores).astype(bf16)
            term = nn(d_scores, q)
            d_k = term if d_k is None else d_k + term
            pt_n[start:start + HEAD, part] = dq_t[:HEAD]
            pt_g[out_at:out_at + HEAD, part] = out_t[:HEAD]
            att[part, h * PAD:(h + 1) * PAD] = out_t.T
        pt_n[start + HEAD:start + 2 * HEAD] = d_k.T[:HEAD].astype(bf16)
        pt_n[start + 2 * HEAD:start + 3 * HEAD] = d_v.T[:HEAD].astype(bf16)

    def chunk(piece, zc):
        block = pl.ds(pl.multiple_of(lax.rem(zc + 2 * nz, nz) * CHUNK, 16), CHUNK)
        if piece == 0:
            a = nn(n_t[block], pn1[...])
            b = nn(go_t[block], pg1[...])
            return jnp.concatenate([a[:, :PAD], a[:, PAD:] + b], axis=1)
        if piece == 1:
            b = nn(go_t[block], pg2[...])
            a = nn(n_t[block], pn2[...])
            last = nn(n_t[block], pn3[...])
            return jnp.concatenate([b[:, :PAD], b[:, PAD:] + a, last], axis=1)

    rs_copies = {}
    mid = CHUNK // 2

    def rs_send(piece, way, step, part):
        index = (piece * 2 + way) * far + step
        rs_copies[piece, way, step] = send(
            rs_out[piece].at[way, step, part], rs_in[piece].at[way, step, part],
            rs_s.at[index], rs_r.at[index], at_z(z + 1) if way == 0 else at_z(z + nz - 1),
        )

    def rs_first(piece):
        value = chunk(piece, z + far).astype(bf16)
        rs_out[piece][0, 0, :mid] = value[:mid]
        rs_out[piece][1, 0, mid:] = value[mid:]
        rs_send(piece, 0, 0, pl.ds(0, mid))
        rs_send(piece, 1, 0, pl.ds(mid, mid))

    def rs_step(piece, step):
        for way in range(2):
            value = chunk(piece, z + far - step if way == 0 else z - far + step)
            rs_copies[piece, way, step - 1].wait_recv()
            if step == 1:
                if way == 0:
                    got = rs_in[piece][0, 0, :mid].astype(f32)
                    value = jnp.concatenate([value[:mid] + got, value[mid:]], axis=0)
                else:
                    got = rs_in[piece][1, 0, mid:].astype(f32)
                    value = jnp.concatenate([value[:mid], value[mid:] + got], axis=0)
            else:
                value = value + rs_in[piece][way, step - 1].astype(f32)
            rs_out[piece][way, step] = value.astype(bf16)
            rs_send(piece, way, step, pl.ds(0, CHUNK))

    per = OWN // NS

    def rs_last(piece):
        value = chunk(piece, z)
        for way in range(2):
            rs_copies[piece, way, far - 1].wait_recv()
            value = value + rs_in[piece][way, far - 1].astype(f32)
        wide = jnp.concatenate([value, jnp.zeros((8, value.shape[1]), f32)], axis=0)
        for i in range(NX * NS):
            fin_out[i, :, PIECES[piece][0]:PIECES[piece][1]] = wide[i * per:i * per + FINAL].astype(bf16)

    fin_copies = {}
    fin_lanes = PIECES

    def fin_send(part):
        low, high = fin_lanes[part]
        for kx in (2, 1, 3, 0):
            for ks in (2, 1, 3, 0):
                if kx or ks:
                    index = NS * kx + ks
                    to = lax.rem(x + kx, NX) * NS + lax.rem(s + ks, NS)
                    device = {"dp": z * NX + lax.rem(x + kx, NX), "seq": lax.rem(s + ks, NS)}
                    fin_copies[part, index] = send(
                        fin_out.at[to, :, pl.ds(low, high - low)],
                        fin_in.at[index, :, pl.ds(low, high - low)],
                        fin_s.at[part * NX * NS + index], fin_r.at[part * NX * NS + index], device,
                    )

    def fin_sum(part):
        low, high = fin_lanes[part]
        for ks in (1, 3, 2, 0):
            total = None
            for kx in range(NX):
                if kx or ks:
                    fin_copies[part, NS * kx + ks].wait_recv()
                    term = fin_in[NS * kx + ks, :, low:high].astype(f32)
                else:
                    term = fin_out[x * NS + s, :, low:high].astype(f32)
                total = term if total is None else total + term
            grads[lax.rem(s + NS - ks, NS), :, low:high] = total

    head(0)
    pn1[...] = pt_n[:256].T
    pg1[...] = pt_g[:PAD].T
    rs_first(0)
    head(1)
    pg2[...] = pt_g[PAD:].T
    pn2[...] = pt_n[3 * PAD:4 * PAD].T
    pn3[...] = pt_n[4 * PAD:].T
    rs_first(1)
    at_copies = [
        send(
            att.at[rows_of(lax.rem(s + k, NS))], att_all.at[s],
            at_s.at[k - 1], at_r.at[k - 1], at_s_(s + k),
        )
        for k in range(1, NS)
    ]
    att_all[s] = att[mine]
    for piece in range(n):
        rs_step(piece, 1)
    for copy in at_copies:
        copy.wait_recv()
    partial_out = nn(att_all[0], wo_pad[:ATT])
    for i in range(1, NS):
        partial_out += nn(att_all[i], wo_pad[i * ATT:(i + 1) * ATT])
    lo_out[...] = partial_out.astype(bf16)
    lo_copy = send(lo_out, lo_in, lo_s, lo_r, other)
    for piece in range(n):
        rs_step(piece, 2)
    lo_copy.wait_recv()
    both = lo_out[...].astype(f32) + lo_in[...].astype(f32)
    layer_out[:, :HALF] = (pk[0].astype(f32) + both[:, :HALF]).astype(bf16)
    layer_out[:, HALF:] = (pk[1].astype(f32) + both[:, HALF:]).astype(bf16)
    for piece in range(n):
        rs_step(piece, 3)
    rs_last(0)
    fin_send(0)
    rs_last(1)
    fin_send(1)
    fin_sum(0)
    fin_sum(1)
    for copy in started:
        if not any(copy is other_copy for other_copy in gone):
            copy.wait_send()


def finish(layer_in, grads, layer_out, qkv, wout):
    per, first, last = OWN // NS, 3 * HEAD, 5 * HEAD
    layer_out[...] = layer_in[...]
    blocks = [grads[i][:per] for i in range(NS)]
    spans = ((0, first), (last, COLS))
    qkv[...] = jnp.concatenate([b[:, low:high] for b in blocks for low, high in spans], axis=1)
    wout[...] = jnp.concatenate([b[:, first:last] for b in blocks], axis=1)


def scratch_shapes(nz):
    far = nz // 2

    def vm(*shape, kind=bf16):
        return pltpu.VMEM(shape, kind)

    def dma(*shape):
        return pltpu.SemaphoreType.DMA(shape)

    one = pltpu.SemaphoreType.DMA
    rings = [vm(2, far, CHUNK, high - low) for low, high in PIECES]
    return [
        vm(1, ROWS // NX, kind=jnp.int32), vm(1, GROUP, kind=jnp.int32), vm(D, kind=f32),
        vm(D, kind=f32),
        vm(ROWS, HALF), vm(ROWS, HALF), vm(2, GROUP, HALF), vm(2, ROWS, HALF), vm(2, GROUP, HALF),
        vm(NS, 8, ROWS, kind=f32), vm(D, HALF), vm(D, 6 * PAD), vm(NS * ATT, D),
        vm(GROUP, 6 * PAD), vm(D, GROUP), vm(D, GROUP), vm(GROUP, ATT), vm(ATT, GROUP),
        vm(GROUP, PAD, kind=f32), vm(COLS, GROUP), vm(3 * PAD, GROUP), vm(GROUP, 2 * PAD),
        vm(GROUP, PAD), vm(GROUP, 2 * PAD), vm(GROUP, PAD), vm(GROUP, PAD), vm(GROUP, ATT),
        vm(NS, ROWS, ATT), vm(ROWS, D), vm(ROWS, D),
        *rings, *rings, vm(NX * NS, FINAL, COLS), vm(NX * NS, FINAL, COLS),
        dma(16), dma(nz - 1), dma(nz - 1), dma(3), dma(3), dma(3), dma(3), dma(3), dma(3),
        dma(3), dma(3), dma(6), dma(6), dma(5), dma(5), dma(3), dma(3), one, one,
        dma(2 * len(PIECES) * far), dma(2 * len(PIECES) * far),
        dma(2 * NX * NS), dma(2 * NX * NS),
    ]


def body(patches, arrivals, segment_ids, norm_gain, norm_bias, w_qkv, w_out, grad_out):
    nz = lax.axis_size("dp") // NX
    anywhere = pl.BlockSpec(memory_space=pl.ANY)
    vmem = pl.BlockSpec(memory_space=pltpu.VMEM)
    layer, grads = pl.pallas_call(
        functools.partial(kernel, nz),
        out_shape=(
            jax.ShapeDtypeStruct((ROWS, D), bf16),
            jax.ShapeDtypeStruct((NS, FINAL, COLS), f32),
        ),
        in_specs=[anywhere] * 8,
        out_specs=(vmem, vmem),
        scratch_shapes=scratch_shapes(nz),
        compiler_params=pltpu.CompilerParams(
            collective_id=0, has_side_effects=True, vmem_limit_bytes=56 * 1024 * 1024
        ),
    )(
        patches, arrivals, segment_ids.reshape(1, GROUP), norm_gain, norm_bias, w_qkv, w_out,
        grad_out,
    )
    per = OWN // NS
    return pl.pallas_call(
        finish,
        out_shape=(
            jax.ShapeDtypeStruct((ROWS, D), bf16),
            jax.ShapeDtypeStruct((per, NS * QKV), f32),
            jax.ShapeDtypeStruct((per, NS * HEADS_OWN * HEAD), f32),
        ),
        in_specs=[vmem, vmem],
        out_specs=(vmem, vmem, vmem),
    )(layer, grads)


def solution(mesh):
    return jax.shard_map(
        body,
        mesh=mesh,
        in_specs=(
            P(("dp", "seq"), None),
            P(("dp", "seq"), None),
            P("dp"),
            P(),
            P(),
            P(None, "tensor"),
            P("tensor", None),
            P(("dp", "seq"), None),
        ),
        out_specs=(P(("dp", "seq"), None), P(("dp", "seq"), "tensor"), P(("dp", "seq"), "tensor")),
        check_vma=False,
    )
```

```python
import functools

import jax
import jax.numpy as jnp
from jax import lax
from jax.experimental import pallas as pl
from jax.experimental.pallas import tpu as pltpu
from jax.sharding import PartitionSpec as P

HEAD = 80
PAD = 128
HEADS_OWN = 2
NX = 4
NS = 4
ROWS = 128
D = 1280
HALF = D // 2
GROUP = NS * ROWS
QKV = 3 * HEADS_OWN * HEAD
ATT = HEADS_OWN * PAD
COLS = 4 * HEADS_OWN * HEAD
PIECES = ((0, 256), (256, 640))
CHUNK = 160
OWN = 40
FINAL = 16
epsilon = 1e-06
big_negative = -1e30
MESH = pl.DeviceIdType.MESH
bf16 = jnp.bfloat16
f32 = jnp.float32


def nn(a, b):
    return jnp.dot(a, b, preferred_element_type=f32)


def nt(a, b):
    return lax.dot_general(a, b, (((1,), (1,)), ((), ())), preferred_element_type=f32)


def iota(shape, axis):
    return lax.broadcasted_iota(jnp.int32, shape, axis)


def kernel(nz, patches, arrivals, seg, gain, bias, w_qkv, w_out, gout, layer_out, grads, *scratch):
    (arrivals_v, seg_v, gain_v, bias_v, az, xs_out, raw, pk, gall, tgt, w_win, w_pad, wo_pad, proj, n_t, go_t, ga, ga_t, segk,
     pt_n, pt_g, pn1, pg1, pg2, pn2, pn3, att, att_all, lo_out, lo_in) = scratch[:30]
    n = len(PIECES)
    rs_out, rs_in = scratch[30:30 + n], scratch[30 + n:30 + 2 * n]
    (fin_out, fin_in, loc, az_s, az_r, gy_s, gy_r, gf_s, gf_r, ax_s, ax_r, tg_s, tg_r, ry_s, ry_r,
     rf_s, rf_r, at_s, at_r, lo_s, lo_r, rs_s, rs_r, fin_s, fin_r) = scratch[30 + 2 * n:]
    dp, s, c = lax.axis_index("dp"), lax.axis_index("seq"), lax.axis_index("tensor")
    z, x = lax.div(dp, NX), lax.rem(dp, NX)
    started, gone = [], []

    def at_z(zt):
        return {"dp": lax.rem(zt + nz, nz) * NX + x}

    def at_x(xt):
        return {"dp": z * NX + lax.rem(xt + NX, NX)}

    def at_s_(st):
        return {"seq": lax.rem(st + NS, NS)}

    other = {"tensor": 1 - c}

    barrier = pltpu.get_barrier_semaphore()
    far = nz // 2
    partners = (
        [at_z(z + k) for k in sorted(range(1, nz), key=lambda k: abs(k - far))]
        + [at_x(x + k) for k in (2, 1, 3)]
        + [at_s_(s + k) for k in (2, 1, 3)]
        + [other]
    )
    for device in partners:
        pl.semaphore_signal(barrier, inc=1, device_id=device, device_id_type=MESH)

    def send(src, dst, ssem, rsem, device):
        copy = pltpu.make_async_remote_copy(
            src_ref=src, dst_ref=dst, send_sem=ssem, recv_sem=rsem, device_id=device,
            device_id_type=MESH,
        )
        copy.start()
        started.append(copy)
        return copy

    def fetch(src, dst, sem):
        copy = pltpu.make_async_copy(src, dst, sem)
        copy.start()
        return copy

    cols = pl.ds(pl.multiple_of(c * HALF, HALF), HALF)
    mine = pl.ds(pl.multiple_of(s * ROWS, ROWS), ROWS)

    own_patch = fetch(
        patches.at[pl.ds(pl.multiple_of(z * 16, 16), 16), cols],
        az.at[pl.ds(pl.multiple_of(z * 16, 16), 16)], loc.at[0],
    )
    small = [
        fetch(a, b, loc.at[12 + i])
        for i, (a, b) in enumerate(
            ((arrivals, arrivals_v), (seg, seg_v), (gain, gain_v), (bias, bias_v))
        )
    ]
    w_start = lax.min(lax.div(QKV * s, 128) * 128, 3 * D // 2 - HALF)
    w_off = QKV * s - w_start
    w_copy = fetch(w_qkv.at[:, pl.ds(pl.multiple_of(w_start, 128), HALF)], w_win, loc.at[3])
    own_gout = [
        fetch(gout.at[:, pl.ds(i * HALF, HALF)], gall.at[i, mine], loc.at[1 + i]) for i in range(2)
    ]
    wo_copies = [
        fetch(w_out.at[pl.ds(i * HEAD, HEAD)], wo_pad.at[pl.ds(i * PAD, HEAD)], loc.at[4 + i])
        for i in range(NS * HEADS_OWN)
    ]
    pl.semaphore_wait(barrier, len(partners))

    az_copies = []
    for k in sorted(range(1, nz), key=lambda k: abs(k - far)):
        zt = lax.rem(z + k, nz)
        az_copies.append(send(
            patches.at[pl.ds(pl.multiple_of(zt * 16, 16), 16), cols],
            az.at[pl.ds(pl.multiple_of(z * 16, 16), 16)],
            az_s.at[k - 1], az_r.at[k - 1], at_z(z + k),
        ))
    gy_copies = {
        k: send(gout.at[:, cols], gall.at[c, mine], gy_s.at[k - 1], gy_r.at[k - 1], at_s_(s + k))
        for k in (1, 3, 2)
    }

    for copy in small:
        copy.wait()

    row, col = iota((ROWS, ROWS), 0), iota((ROWS, ROWS), 1)
    to_x = (x + (row >> 5)) & (NX - 1)
    perm = (col == ((row >> 2) & 7) * 16 + to_x * 4 + (row & 3)).astype(bf16)
    slot = iota((32, ROWS), 1)
    origin = ((slot >> 2) & 7) * NX + ((x + (slot >> 5)) & (NX - 1))
    counter = iota((32, ROWS), 0)
    counts = jnp.broadcast_to(arrivals_v[...].astype(f32), (16, 32)).astype(bf16)
    starts = nn(counts, (counter < origin).astype(bf16))[0:8]
    number = nn(counts, (counter == origin).astype(bf16))[0:8]
    place = (iota((8, ROWS), 1) & 3).astype(f32)
    tgt[s] = jnp.where(place < number, starts + place, -1.0)
    tg_copies = {
        k: send(tgt.at[s], tgt.at[s], tg_s.at[k - 1], tg_r.at[k - 1], at_s_(s + k))
        for k in (1, 3, 2)
    }

    ids = seg_v[...].astype(f32)
    key_ids = jnp.where(ids < 0.0, -2.0, ids)
    segk[...] = jnp.broadcast_to(key_ids, (PAD, GROUP)).T

    for i in range(NS * HEADS_OWN):
        wo_pad[i * PAD + HEAD:(i + 1) * PAD] = jnp.zeros((PAD - HEAD, D), bf16)
    pt_n[3 * HEAD:5 * HEAD] = jnp.zeros((2 * HEAD, GROUP), bf16)
    pt_g[...] = jnp.zeros(pt_g.shape, bf16)

    w_copy.wait()

    def pad_pair(i, carry):
        r, cc = iota((HALF, 2 * PAD), 0), iota((HALF, 2 * PAD), 1)
        d = cc & (PAD - 1)
        wanted = w_off + (2 * i + (cc >> 7)) * HEAD + d
        chosen = ((r == wanted) & (d < HEAD)).astype(bf16)
        out = pl.ds(pl.multiple_of(i * 2 * PAD, 2 * PAD), 2 * PAD)
        w_pad[:, out] = nn(w_win[...], chosen).astype(bf16)
        return carry

    lax.fori_loop(0, 3, pad_pair, 0)

    own_patch.wait()
    for copy in az_copies:
        copy.wait_recv()
    xs = nn(perm, az[...]).astype(bf16)
    quarter = ROWS // NX
    xs_out[...] = xs
    raw[c, pl.ds(pl.multiple_of(s * ROWS, ROWS), quarter)] = xs[:quarter]
    ax_copies = []
    for k in (1, 3, 2):
        landing = pl.multiple_of(s * ROWS + (NX - k) * quarter, quarter)
        ax_copies.append(send(
            xs_out.at[pl.ds(k * quarter, quarter)], raw.at[c, pl.ds(landing, quarter)],
            ax_s.at[k - 1], ax_r.at[k - 1], at_x(x + k),
        ))
    first = pl.ds(pl.multiple_of(s * ROWS, ROWS), quarter)
    rest = pl.ds(pl.multiple_of(s * ROWS + quarter, quarter), ROWS - quarter)
    ry_copies, rf_copies = {}, {}

    def spread(part, block):
        for k in (1, 3, 2):
            ry_copies[part, k] = send(
                raw.at[c, block], raw.at[c, block], ry_s.at[3 * part + k - 1],
                ry_r.at[3 * part + k - 1], at_s_(s + k),
            )
        rf_copies[part] = send(
            raw.at[c, block], raw.at[c, block], rf_s.at[part], rf_r.at[part], other
        )

    spread(0, first)
    for copy in ax_copies:
        copy.wait_recv()
    spread(1, rest)

    def peer(k):
        return lax.rem(s + NS - k, NS)

    def rows_of(index):
        return pl.ds(pl.multiple_of(index * ROWS, ROWS), ROWS)

    def take(index, later=False):
        block = rows_of(index)
        pick = (row.astype(f32) == tgt[index][0:1]).astype(bf16)
        x0, x1 = nn(pick, raw[0, block]), nn(pick, raw[1, block])
        y0, y1 = x0, x1
        mean = (jnp.sum(x0, axis=1, keepdims=True) + jnp.sum(x1, axis=1, keepdims=True)) / D
        x0, x1 = x0 - mean, x1 - mean
        var = (jnp.sum(x0 * x0, axis=1, keepdims=True) + jnp.sum(x1 * x1, axis=1, keepdims=True)) / D
        inv = lax.rsqrt(var + epsilon)
        gains, biases = gain_v[...].reshape(1, D), bias_v[...].reshape(1, D)
        x0 = (x0 * inv * gains[:, :HALF] + biases[:, :HALF]).astype(bf16)
        x1 = (x1 * inv * gains[:, HALF:] + biases[:, HALF:]).astype(bf16)
        proj[block] = (nn(x0, w_pad[:HALF]) + nn(x1, w_pad[HALF:])).astype(bf16)
        if not later:
            n_t[:HALF, block] = x0.T
            n_t[HALF:, block] = x1.T
            return y0, y1
        return block, x0, x1

    gf_copies = []
    for k in (1, 3, 2):
        gy_copies[k].wait_recv()
        block = rows_of(peer(k))
        gf_copies.append(send(
            gall.at[c, block], gall.at[c, block], gf_s.at[k - 1], gf_r.at[k - 1], other
        ))
    for part in range(2):
        rf_copies[part].wait_recv()
    own0, own1 = take(s)
    pk[0] = own0.astype(bf16)
    pk[1] = own1.astype(bf16)
    for copy in wo_copies:
        copy.wait()
    for copy in own_gout:
        copy.wait()
    for copy in gf_copies:
        copy.wait_recv()
    wo_mine = wo_pad[pl.ds(pl.multiple_of(s * ATT, ATT), ATT)]
    ga[...] = (nt(gall[0], wo_mine[:, :HALF]) + nt(gall[1], wo_mine[:, HALF:])).astype(bf16)
    ga_t[...] = (nt(wo_mine[:, :HALF], gall[0]) + nt(wo_mine[:, HALF:], gall[1])).astype(bf16)

    def pass_on(k):
        for part in range(2):
            ry_copies[part, k].wait_recv()
        tg_copies[k].wait_recv()
        block = rows_of(peer(k))
        rf_copies[1 + k] = send(
            raw.at[c, block], raw.at[c, block], rf_s.at[1 + k], rf_r.at[1 + k], other
        )

    def take_peer(k, later=False):
        rf_copies[1 + k].wait_recv()
        return take(peer(k), later)

    pass_on(1)
    pass_on(3)
    pass_on(2)
    take_peer(1)
    take_peer(3)
    go_t[:HALF] = gall[0].T
    go_t[HALF:] = gall[1].T
    block, n0, n1 = take_peer(2, later=True)

    scale = HEAD ** (-0.5)
    to_exp2 = scale * 1.4426950408889634
    query_ids = ids

    def head(h):
        base = 3 * PAD * h
        k_, v_ = proj[:, base + PAD:base + 2 * PAD], proj[:, base + 2 * PAD:base + 3 * PAD]
        k_t, v_t = k_.T, v_.T
        wide = 256
        parts = [slice(b * wide, (b + 1) * wide) for b in range(GROUP // wide)]
        keys = jnp.concatenate([segk[...]] * (wide // PAD), axis=1)
        q_ = [proj[part, base:base + PAD] for part in parts]
        g_ = [ga[part, h * PAD:(h + 1) * PAD] for part in parts]
        scores = [nt(k_, q) for q in q_]
        d_weights = [nt(v_, g) for g in g_]
        raised, share = [], []
        for part, score in zip(parts, scores):
            masked = jnp.where(keys == query_ids[:, part], score, big_negative)
            top = jnp.max(masked, axis=0, keepdims=True)
            up = jnp.exp2((masked - top) * to_exp2)
            total = jnp.sum(up, axis=0, keepdims=True)
            raised.append(up)
            share.append(jnp.where(query_ids[:, part] < 0.0, 0.0, 1.0 / total))
        d_k = d_v = None
        start = 0 if h == 0 else 5 * HEAD
        out_at = 3 * HEAD - PAD + h * HEAD
        for part, q, g, up, sh, dw in zip(parts, q_, g_, raised, share, d_weights):
            g_t = ga_t[h * PAD:(h + 1) * PAD, part]
            exact = up * sh
            weights = exact.astype(bf16)
            out_t = nn(v_t, weights).astype(bf16)
            term = nn(weights, g)
            d_v = term if d_v is None else d_v + term
            delta = jnp.sum(g_t.astype(f32) * out_t.astype(f32), axis=0, keepdims=True)
            d_scores = (exact * (dw - delta) * scale).astype(bf16)
            dq_t = nn(k_t, d_scores).astype(bf16)
            term = nn(d_scores, q)
            d_k = term if d_k is None else d_k + term
            pt_n[start:start + HEAD, part] = dq_t[:HEAD]
            pt_g[out_at:out_at + HEAD, part] = out_t[:HEAD]
            att[part, h * PAD:(h + 1) * PAD] = out_t.T
        pt_n[start + HEAD:start + 2 * HEAD] = d_k.T[:HEAD].astype(bf16)
        pt_n[start + 2 * HEAD:start + 3 * HEAD] = d_v.T[:HEAD].astype(bf16)

    def chunk(piece, zc):
        block = pl.ds(pl.multiple_of(lax.rem(zc + 2 * nz, nz) * CHUNK, 16), CHUNK)
        if piece == 0:
            a = nn(n_t[block], pn1[...])
            b = nn(go_t[block], pg1[...])
            return jnp.concatenate([a[:, :PAD], a[:, PAD:] + b], axis=1)
        if piece == 1:
            b = nn(go_t[block], pg2[...])
            a = nn(n_t[block], pn2[...])
            last = nn(n_t[block], pn3[...])
            return jnp.concatenate([b[:, :PAD], b[:, PAD:] + a, last], axis=1)

    rs_copies = {}
    mid = CHUNK // 2

    def rs_send(piece, way, step, part):
        index = (piece * 2 + way) * far + step
        rs_copies[piece, way, step] = send(
            rs_out[piece].at[way, step, part], rs_in[piece].at[way, step, part],
            rs_s.at[index], rs_r.at[index], at_z(z + 1) if way == 0 else at_z(z + nz - 1),
        )

    def rs_first(piece):
        value = chunk(piece, z + far).astype(bf16)
        rs_out[piece][0, 0, :mid] = value[:mid]
        rs_out[piece][1, 0, mid:] = value[mid:]
        rs_send(piece, 0, 0, pl.ds(0, mid))
        rs_send(piece, 1, 0, pl.ds(mid, mid))

    def rs_step(piece, step):
        for way in range(2):
            value = chunk(piece, z + far - step if way == 0 else z - far + step)
            rs_copies[piece, way, step - 1].wait_recv()
            if step == 1:
                if way == 0:
                    got = rs_in[piece][0, 0, :mid].astype(f32)
                    value = jnp.concatenate([value[:mid] + got, value[mid:]], axis=0)
                else:
                    got = rs_in[piece][1, 0, mid:].astype(f32)
                    value = jnp.concatenate([value[:mid], value[mid:] + got], axis=0)
            else:
                value = value + rs_in[piece][way, step - 1].astype(f32)
            rs_out[piece][way, step] = value.astype(bf16)
            rs_send(piece, way, step, pl.ds(0, CHUNK))

    per = OWN // NS

    def rs_last(piece):
        value = chunk(piece, z)
        for way in range(2):
            rs_copies[piece, way, far - 1].wait_recv()
            value = value + rs_in[piece][way, far - 1].astype(f32)
        wide = jnp.concatenate([value, jnp.zeros((8, value.shape[1]), f32)], axis=0)
        for i in range(NX * NS):
            fin_out[i, :, PIECES[piece][0]:PIECES[piece][1]] = wide[i * per:i * per + FINAL].astype(bf16)

    fin_copies = {}
    fin_lanes = PIECES

    def fin_send(part):
        low, high = fin_lanes[part]
        for kx in (2, 1, 3, 0):
            for ks in (2, 1, 3, 0):
                if kx or ks:
                    index = NS * kx + ks
                    to = lax.rem(x + kx, NX) * NS + lax.rem(s + ks, NS)
                    device = {"dp": z * NX + lax.rem(x + kx, NX), "seq": lax.rem(s + ks, NS)}
                    fin_copies[part, index] = send(
                        fin_out.at[to, :, pl.ds(low, high - low)],
                        fin_in.at[index, :, pl.ds(low, high - low)],
                        fin_s.at[part * NX * NS + index], fin_r.at[part * NX * NS + index], device,
                    )

    def fin_sum(part):
        low, high = fin_lanes[part]
        for ks in (1, 3, 2, 0):
            total = None
            for kx in range(NX):
                if kx or ks:
                    fin_copies[part, NS * kx + ks].wait_recv()
                    term = fin_in[NS * kx + ks, :, low:high].astype(f32)
                else:
                    term = fin_out[x * NS + s, :, low:high].astype(f32)
                total = term if total is None else total + term
            grads[lax.rem(s + NS - ks, NS), :, low:high] = total

    head(0)
    n_t[:HALF, block] = n0.T
    n_t[HALF:, block] = n1.T
    pn1[...] = pt_n[:256].T
    pg1[...] = pt_g[:PAD].T
    rs_first(0)
    head(1)
    pg2[...] = pt_g[PAD:].T
    pn2[...] = pt_n[3 * PAD:4 * PAD].T
    pn3[...] = pt_n[4 * PAD:].T
    rs_first(1)
    at_copies = [
        send(
            att.at[rows_of(lax.rem(s + k, NS))], att_all.at[s],
            at_s.at[k - 1], at_r.at[k - 1], at_s_(s + k),
        )
        for k in range(1, NS)
    ]
    att_all[s] = att[mine]
    for piece in range(n):
        rs_step(piece, 1)
    for copy in at_copies:
        copy.wait_recv()
    partial_out = nn(att_all[0], wo_pad[:ATT])
    for i in range(1, NS):
        partial_out += nn(att_all[i], wo_pad[i * ATT:(i + 1) * ATT])
    lo_out[...] = partial_out.astype(bf16)
    lo_copy = send(lo_out, lo_in, lo_s, lo_r, other)
    for piece in range(n):
        rs_step(piece, 2)
    lo_copy.wait_recv()
    both = lo_out[...].astype(f32) + lo_in[...].astype(f32)
    layer_out[:, :HALF] = (pk[0].astype(f32) + both[:, :HALF]).astype(bf16)
    layer_out[:, HALF:] = (pk[1].astype(f32) + both[:, HALF:]).astype(bf16)
    for piece in range(n):
        rs_step(piece, 3)
    rs_last(0)
    fin_send(0)
    rs_last(1)
    fin_send(1)
    fin_sum(0)
    fin_sum(1)
    for copy in started:
        if not any(copy is other_copy for other_copy in gone):
            copy.wait_send()


def finish(layer_in, grads, layer_out, qkv, wout):
    per, first, last = OWN // NS, 3 * HEAD, 5 * HEAD
    layer_out[...] = layer_in[...]
    blocks = [grads[i][:per] for i in range(NS)]
    spans = ((0, first), (last, COLS))
    qkv[...] = jnp.concatenate([b[:, low:high] for b in blocks for low, high in spans], axis=1)
    wout[...] = jnp.concatenate([b[:, first:last] for b in blocks], axis=1)


def scratch_shapes(nz):
    far = nz // 2

    def vm(*shape, kind=bf16):
        return pltpu.VMEM(shape, kind)

    def dma(*shape):
        return pltpu.SemaphoreType.DMA(shape)

    one = pltpu.SemaphoreType.DMA
    rings = [vm(2, far, CHUNK, high - low) for low, high in PIECES]
    return [
        vm(1, ROWS // NX, kind=jnp.int32), vm(1, GROUP, kind=jnp.int32), vm(D, kind=f32),
        vm(D, kind=f32),
        vm(ROWS, HALF), vm(ROWS, HALF), vm(2, GROUP, HALF), vm(2, ROWS, HALF), vm(2, GROUP, HALF),
        vm(NS, 8, ROWS, kind=f32), vm(D, HALF), vm(D, 6 * PAD), vm(NS * ATT, D),
        vm(GROUP, 6 * PAD), vm(D, GROUP), vm(D, GROUP), vm(GROUP, ATT), vm(ATT, GROUP),
        vm(GROUP, PAD, kind=f32), vm(COLS, GROUP), vm(3 * PAD, GROUP), vm(GROUP, 2 * PAD),
        vm(GROUP, PAD), vm(GROUP, 2 * PAD), vm(GROUP, PAD), vm(GROUP, PAD), vm(GROUP, ATT),
        vm(NS, ROWS, ATT), vm(ROWS, D), vm(ROWS, D),
        *rings, *rings, vm(NX * NS, FINAL, COLS), vm(NX * NS, FINAL, COLS),
        dma(16), dma(nz - 1), dma(nz - 1), dma(3), dma(3), dma(3), dma(3), dma(3), dma(3),
        dma(3), dma(3), dma(6), dma(6), dma(5), dma(5), dma(3), dma(3), one, one,
        dma(2 * len(PIECES) * far), dma(2 * len(PIECES) * far),
        dma(2 * NX * NS), dma(2 * NX * NS),
    ]


def body(patches, arrivals, segment_ids, norm_gain, norm_bias, w_qkv, w_out, grad_out):
    nz = lax.axis_size("dp") // NX
    anywhere = pl.BlockSpec(memory_space=pl.ANY)
    vmem = pl.BlockSpec(memory_space=pltpu.VMEM)
    layer, grads = pl.pallas_call(
        functools.partial(kernel, nz),
        out_shape=(
            jax.ShapeDtypeStruct((ROWS, D), bf16),
            jax.ShapeDtypeStruct((NS, FINAL, COLS), f32),
        ),
        in_specs=[anywhere] * 8,
        out_specs=(vmem, vmem),
        scratch_shapes=scratch_shapes(nz),
        compiler_params=pltpu.CompilerParams(
            collective_id=0, has_side_effects=True, vmem_limit_bytes=56 * 1024 * 1024
        ),
    )(
        patches, arrivals, segment_ids.reshape(1, GROUP), norm_gain, norm_bias, w_qkv, w_out,
        grad_out,
    )
    per = OWN // NS
    return pl.pallas_call(
        finish,
        out_shape=(
            jax.ShapeDtypeStruct((ROWS, D), bf16),
            jax.ShapeDtypeStruct((per, NS * QKV), f32),
            jax.ShapeDtypeStruct((per, NS * HEADS_OWN * HEAD), f32),
        ),
        in_specs=[vmem, vmem],
        out_specs=(vmem, vmem, vmem),
    )(layer, grads)


def solution(mesh):
    return jax.shard_map(
        body,
        mesh=mesh,
        in_specs=(
            P(("dp", "seq"), None),
            P(("dp", "seq"), None),
            P("dp"),
            P(),
            P(),
            P(None, "tensor"),
            P("tensor", None),
            P(("dp", "seq"), None),
        ),
        out_specs=(P(("dp", "seq"), None), P(("dp", "seq"), "tensor"), P(("dp", "seq"), "tensor")),
        check_vma=False,
    )
```
